256 devices in a mesh: region: 256 (over y, x, z, core).
Axes of the slice: x: 4, y: 4, z: 8, core: 2. Of those that a mesh axis runs over, the one named last changes fastest.
Arguments:
- pixels: bfloat16 [1024, 512, 2, 256], P('region'), may hold values from -6 to 6
- leaf_valid: int32 [1024, 512], P('region'), may hold values 0 or 1
- leaf_basis: bfloat16 [256, 32], replicated, may hold values from -0.75 to 0.75
- near_blocks: bfloat16 [9, 256, 256], replicated, may hold values from -0.125 to 0.125
- transfer: float32 [2, 32, 32], replicated, may hold values from -1 to 1
- leaf_coupling: float32 [40, 32, 32], replicated, may hold values from -0.078125 to 0.078125
- top_coupling: float32 [160, 32, 32], replicated, may hold values from -0.001953125 to 0.001953125
- top_partner: int32 [480, 8], replicated, may hold values from 0 to 479, as said below
- top_offset: int32 [480, 8], replicated, may hold values from 0 to 159
- top_count: int32 [480], replicated, may hold values from 1 to 8
Outputs:
- covariance_product: float32 [1024, 512, 2, 256], P('region')
The draws below stay inside these ranges and needn't reach their ends.
Inputs may be any that keep to these rules, and one draw needn't show every extreme that they name: `top_partner`: rows 0 to 256 - 1 are the band nodes, then each level above takes half as many rows; every entry names a node of its row's own level, two or more places away from the row's node in that level's cyclic order.
All inputs are finite; a program needn't handle non-finite values. No bound on the sum of `leaf_valid` on one device may be relied on, other than what follows from the above.
Results may differ from the reference program's by a relative error of at most 0.0003.
Values may be sent and summed in bfloat16 or wider, within the bound.
A program may use at most 256 MiB of HBM per device.

```python
import jax
import jax.numpy as jnp
from jax import lax

LEAF = 256
RANK = 32
RHS = 2
BY = 4
BX = 512
PT = 8
TOP_OFF = 160
LEAF_ROWS = 1024
TOP_NODES = 480


def draw_top_partner(key, part):
    key = jax.random.fold_in(key, 11)
    regions = TOP_NODES * 8 // 15
    row_ids = jnp.arange(TOP_NODES, dtype=jnp.int32)
    height = (row_ids >= regions).astype(jnp.int32) + (row_ids >= regions + regions // 2).astype(jnp.int32) + (row_ids >= regions + regions // 2 + regions // 4).astype(jnp.int32)
    node_count = jnp.right_shift(jnp.full((TOP_NODES,), regions, jnp.int32), height)
    node_base = 2 * regions - 2 * node_count
    local_ids = row_ids - node_base
    stride = jax.random.randint(key, (TOP_NODES, PT), 0, 1 << 20) % (node_count - 3)[:, None] + 2
    return (node_base[:, None] + (local_ids[:, None] + stride) % node_count[:, None]).astype(jnp.int32)


def draw_top_count(key, part):
    key = jax.random.fold_in(key, 23)
    counts = jax.random.randint(key, (TOP_NODES,), 1, PT + 1)
    return counts.at[0].set(PT).astype(jnp.int32)


def plant(values, own_key, low, top_value):
    shape = values.shape
    spot = [jax.random.randint(jax.random.fold_in(own_key, axis), (), 0, shape[axis]) for axis in range(len(shape))]
    values = values.at[tuple(spot)].set(low)
    longest = shape.index(max(shape))
    spot[longest] = (spot[longest] + 1) % shape[longest]
    return values.at[tuple(spot)].set(top_value)


def shard_levels(stream_key, extent, shards, least, high):
    loudness = 1.0
    for axis_at, shards_of in shards:
        steps = jax.random.uniform(jax.random.fold_in(jax.random.fold_in(stream_key, 6), axis_at), (shards_of,), jnp.float32, least / len(shards), high / len(shards))
        loudness = loudness * jnp.repeat(jnp.exp(steps), extent[axis_at] // shards_of).reshape((-1,) + (1,) * (len(extent) - 1 - axis_at))
    return loudness


def centred(stream_key, extent, scale, limit, cuts=(), kind=jnp.bfloat16):
    drawn = jax.random.normal(stream_key, extent, jnp.float32) * scale
    if len(cuts) > 0:
        drawn = shard_levels(stream_key, extent, cuts, -0.22, 0.18) * drawn
    return jnp.clip(drawn, min=-limit, max=limit).astype(kind)


def setup_inputs(seed: int = 0) -> dict:
    key_list = jax.random.split(jax.random.key(seed), 11)
    return {
        "pixels": centred(key_list[0], (LEAF_ROWS, BX, RHS, LEAF), 1.0, 6.0, ((0, 256),)),
        "leaf_valid": plant((jax.random.randint(key_list[1], (LEAF_ROWS, BX), 0, 4) < 3).astype(jnp.int32), jax.random.fold_in(key_list[1], 1), 0, 1),
        "leaf_basis": centred(key_list[2], (LEAF, RANK), (LEAF // 4) ** -0.5, 0.75),
        "near_blocks": centred(key_list[3], (9, LEAF, LEAF), (9 * LEAF) ** -0.5, 0.125),
        "transfer": centred(key_list[4], (2, RANK, RANK), RANK ** -0.5, 1.0, (), jnp.float32),
        "leaf_coupling": centred(key_list[5], (40, RANK, RANK), (160 * RANK) ** -0.5, 0.078125, (), jnp.float32),
        "top_coupling": centred(key_list[6], (TOP_OFF, RANK, RANK), (16 * RANK * PT * BY * BX) ** -0.5, 0.001953125, (), jnp.float32),
        "top_partner": draw_top_partner(jax.random.fold_in(key_list[10], 71), 0),
        "top_offset": plant(jax.random.randint(key_list[8], (TOP_NODES, PT), 0, TOP_OFF), jax.random.fold_in(key_list[8], 1), 0, TOP_OFF - 1).astype(jnp.int32),
        "top_count": draw_top_count(jax.random.fold_in(key_list[10], 71), 0),
    }


def leaf_coefs(masked, leaf_basis):
    return jnp.dot(masked, leaf_basis, preferred_element_type=jnp.float32)


def merge_pair(lower_half, upper_half, transfer):
    return (jnp.dot(lower_half, transfer[0], precision=lax.Precision.HIGHEST)
            + jnp.dot(upper_half, transfer[1], precision=lax.Precision.HIGHEST))


def split_pair(parent, transfer):
    lower_half = jnp.dot(parent, transfer[0].T, precision=lax.Precision.HIGHEST)
    upper_half = jnp.dot(parent, transfer[1].T, precision=lax.Precision.HIGHEST)
    return lower_half, upper_half


def climb_tree(coef, transfer):
    level_now = coef
    while level_now.shape[0] > 1:
        halves = level_now.reshape((level_now.shape[0] // 2, 2) + level_now.shape[1:])
        level_now = merge_pair(halves[:, 0], halves[:, 1], transfer)
    while level_now.shape[1] > 1:
        halves = level_now.reshape((1, level_now.shape[1] // 2, 2) + level_now.shape[2:])
        level_now = merge_pair(halves[:, :, 0], halves[:, :, 1], transfer)
    return level_now[0, 0]


def descend(root_exp, transfer, band_rows, band_cols):
    level_now = root_exp[None, None]
    while level_now.shape[1] < band_cols:
        lower_half, upper_half = split_pair(level_now, transfer)
        level_now = jnp.stack([lower_half, upper_half], 2).reshape((1, 2 * level_now.shape[1]) + level_now.shape[2:])
    while level_now.shape[0] < band_rows:
        lower_half, upper_half = split_pair(level_now, transfer)
        level_now = jnp.stack([lower_half, upper_half], 1).reshape((2 * level_now.shape[0],) + level_now.shape[1:])
    return level_now


def near_field(extended, near_blocks, band_rows):
    band_cols = extended.shape[1]
    padded = jnp.pad(extended, ((0, 0), (1, 1), (0, 0), (0, 0)))
    accumulated = jnp.zeros((band_rows,) + extended.shape[1:], jnp.float32)
    for row_shift in range(3):
        for col_shift in range(3):
            shifted = padded[row_shift:row_shift + band_rows, col_shift:col_shift + band_cols]
            accumulated = accumulated + jnp.dot(shifted, near_blocks[3 * row_shift + col_shift], preferred_element_type=jnp.float32)
    return accumulated


def cycle_columns(row_shift):
    return [column for column in range(7) if max(abs(row_shift - 3), abs(column - 3)) >= 2]


def leaf_far(coef_ext, coupling, band_rows):
    band_cols = coef_ext.shape[1]
    padded = jnp.pad(coef_ext, ((0, 0), (3, 3), (0, 0), (0, 0)))
    accumulated = jnp.zeros((band_rows,) + coef_ext.shape[1:], jnp.float32)
    first_id = 0
    for row_shift in range(7):
        columns = cycle_columns(row_shift)
        cycle_views = jnp.concatenate([padded[row_shift:row_shift + band_rows, column:column + band_cols] for column in columns], axis=-1)
        stacked = coupling[first_id:first_id + len(columns)].reshape(len(columns) * coupling.shape[1], coupling.shape[2])
        accumulated = accumulated + jnp.dot(cycle_views, stacked, precision=lax.Precision.HIGHEST)
        first_id = first_id + len(columns)
    return accumulated


def node_local(node_table, partners, offsets, counts, top_coupling):
    slot_ids = jnp.arange(partners.shape[-1], dtype=jnp.int32)
    live_slots = (slot_ids[None, :] < counts[:, None]).astype(jnp.float32)
    picked = node_table[partners] * live_slots[:, :, None, None]
    blocks = top_coupling[offsets]
    return jnp.einsum('npab,npbc->nac', picked, blocks, precision=lax.Precision.HIGHEST)


def top_levels(region_table, transfer):
    levels_list = [region_table]
    for height in range(3):
        halves = levels_list[-1].reshape((-1, 2) + region_table.shape[1:])
        levels_list.append(merge_pair(halves[:, 0], halves[:, 1], transfer))
    return jnp.concatenate(levels_list, 0)


def reference(pixels, leaf_valid, leaf_basis, near_blocks, transfer, leaf_coupling, top_coupling, top_partner, top_offset, top_count):
    all_rows, band_cols = pixels.shape[0], pixels.shape[1]
    regions = all_rows // BY
    masked = pixels * leaf_valid.astype(jnp.bfloat16)[:, :, None, None]
    pixel_pad = jnp.pad(masked, ((3, 3), (0, 0), (0, 0), (0, 0)))
    band_ids = jnp.arange(regions, dtype=jnp.int32)

    def band_extended(band_index):
        start_row = (band_index * BY).astype(jnp.int32)
        return lax.dynamic_slice_in_dim(pixel_pad, start_row, BY + 6, 0)

    def climb_band(band_index):
        own_rows = band_extended(band_index)[3:3 + BY]
        return climb_tree(leaf_coefs(own_rows, leaf_basis), transfer)

    region_table = lax.map(climb_band, band_ids)
    node_table = top_levels(region_table, transfer)
    local_all = node_local(node_table, top_partner, top_offset, top_count, top_coupling)
    node_bases = [0, regions, regions + regions // 2, regions + regions // 2 + regions // 4]
    expansion = local_all[node_bases[3]:node_bases[3] + regions // 8]
    for height in (2, 1, 0):
        lower_half, upper_half = split_pair(expansion, transfer)
        children = jnp.stack([lower_half, upper_half], 1).reshape((-1,) + expansion.shape[1:])
        expansion = local_all[node_bases[height]:node_bases[height] + regions // (2 ** height)] + children

    def band_out(band_index):
        start_row = (band_index * BY).astype(jnp.int32)
        extended = band_extended(band_index)
        coef_ext = leaf_coefs(extended, leaf_basis)
        near_part = near_field(extended[2:BY + 4], near_blocks, BY)
        far_part = leaf_far(coef_ext, leaf_coupling, BY)
        root_exp = lax.dynamic_index_in_dim(expansion, band_index, 0, keepdims=False)
        leaf_exp = descend(root_exp, transfer, BY, band_cols) + far_part
        field_out = near_part + jnp.dot(leaf_exp, leaf_basis.astype(jnp.float32).T, precision=lax.Precision.HIGHEST)
        validity = lax.dynamic_slice_in_dim(leaf_valid, start_row, BY, 0).astype(jnp.float32)
        return field_out * validity[:, :, None, None]

    banded = lax.map(band_out, band_ids)
    return banded.reshape((all_rows,) + banded.shape[2:])
```

```python
import functools

import jax
import jax.numpy as jnp
from jax import lax
from jax.experimental import pallas as pl
from jax.experimental.pallas import tpu as pltpu
from jax.sharding import PartitionSpec as P

MESH = pl.DeviceIdType.MESH
F32 = jnp.float32
BF16 = jnp.bfloat16
NN = (((1,), (0,)), ((), ()))
NT = (((1,), (1,)), ((), ()))
IN_ORDER = (1, 2, 0, 3)
VMEM_LIMIT = 56 << 20


def dot(a, b, dims=NN):
    return lax.dot_general(a, b, dims, preferred_element_type=F32)


def split(x):
    hi = x.astype(BF16)
    return hi, (x - hi.astype(F32)).astype(BF16)


def dot3(a, b, dims=NN):
    a_hi, a_lo = split(a)
    b_hi, b_lo = split(b)
    return dot(a_hi, b_hi, dims) + (dot(a_lo, b_hi, dims) + dot(a_hi, b_lo, dims))


def iota(shape, axis):
    return lax.broadcasted_iota(jnp.int32, shape, axis)


def tree_paths(transfer):
    side0, side1 = transfer[0], transfer[1]
    both = jnp.concatenate([side0, side1], 0)
    lanes = jnp.concatenate([side0, side1], 1)
    pairs = dot3(both, lanes)
    two = jnp.concatenate([pairs[:, :32], pairs[:, 32:]], 0)
    three = dot3(two, lanes)
    three = jnp.concatenate([three[:, :32], three[:, 32:]], 0)
    two_lanes = jnp.concatenate([two[32 * s : 32 * s + 32] for s in range(4)], 1)
    four = dot3(two, two_lanes)
    four = jnp.concatenate([four[:, 32 * s : 32 * s + 32] for s in range(4)], 0)
    return both, two, three, four


def mask_rows(valid):
    values = valid.astype(F32).astype(BF16)
    values = jnp.concatenate([values, values], 0)
    lane = iota((512, 1024), 1)
    leaf = (lane & 510) + (lane >> 9)
    pick = (iota((512, 1024), 0) == leaf).astype(F32).astype(BF16)
    return dot(values, pick)


def column(row):
    return jnp.concatenate(
        [jnp.broadcast_to(row[:, 128 * b : 128 * b + 128], (128, 128)).T for b in range(4)], 0
    )


def climb(packed, v_ref, w_ref, paths):
    _, _, three, four = paths
    merge = jnp.concatenate(
        [three[(c * 4 + i) * 32 : (c * 4 + i) * 32 + 32] for i in IN_ORDER for c in range(2)], 0
    )
    v_ref[:, 0:32] = dot3(packed, merge)
    rows = []
    for rhs in range(2):
        rows.append(
            jnp.concatenate(
                [v_ref[pl.ds(2 * b + rhs, 16, stride=32), :][:, 0:32] for b in range(16)], 1
            )
        )
    w_ref[:, 0:32] = dot3(jnp.concatenate(rows, 0), four)
    last = jnp.concatenate([w_ref[pl.ds(a, 2, stride=16), :][:, 0:32] for a in range(16)], 1)
    return dot3(jnp.concatenate([last, last, last, last], 0), four)[0:2]


def kernel_up(x, valid, bt, transfer, xm, mcol, packed, region, xs, basis, v_ref, w_ref, sem):
    copies = []
    for i in range(4):
        for c in range(2):
            for lt in range(2):
                copy = pltpu.make_async_copy(
                    x.at[i, :, c, :, pl.ds(lt * 128, 128)], xs.at[i, c, lt], sem.at[i, c, lt]
                )
                copy.start()
                copies.append(copy)
    basis[...] = jnp.zeros_like(basis)
    for at, i in enumerate(IN_ORDER):
        for c in range(2):
            basis[pl.ds(at * 64 + c * 32, 32), pl.ds((i * 2 + c) * 256, 256)] = bt[...]
    paths = tree_paths(transfer)
    rows = mask_rows(valid[...])
    for i in range(4):
        for c in range(2):
            col = column(rows[i : i + 1, c * 512 : c * 512 + 512]).astype(BF16)
            mcol[i, c] = col
            for lt in range(2):
                copies[(i * 2 + c) * 2 + lt].wait()
                part = xs.at[i, c, lt].reshape(512, 128)[...]
                xm[i, c, :, lt * 128 : lt * 128 + 128] = part * col
    pixels = jnp.concatenate([xm[i, c] for i in range(4) for c in range(2)], 1)
    packed[...] = dot(pixels, basis[...], NT)
    top = climb(packed[...], v_ref, w_ref, paths)
    region[0] = jnp.concatenate([top[0:1], top[1:2], jnp.zeros((1, 64), F32)], 1)


def kernel_move(n, xm, packed, region, hx, hc, table, px_s, px_r, cf_s, cf_r, g1_s, g1_r, g2_s, g2_r, own):
    me = lax.axis_index("region")
    right, left = lax.rem(me + 1, n), lax.rem(me + n - 1, n)
    group = me // 16
    spot = lax.rem(me, 16)
    groups = n // 16
    barrier = pltpu.get_barrier_semaphore()
    peers1 = [group * 16 + lax.rem(spot + k, 16) for k in range(1, 16)]
    peers2 = [lax.rem(group + k, groups) * 16 + spot for k in range(1, groups)]
    for peer in [left, right] + peers1 + peers2:
        pl.semaphore_signal(barrier, inc=1, device_id=(peer,), device_id_type=MESH)
    pl.semaphore_wait(barrier, 2 + 15 + groups - 1)

    def remote(src, dst, send, recv, peer):
        copy = pltpu.make_async_remote_copy(
            src_ref=src, dst_ref=dst, send_sem=send, recv_sem=recv, device_id=(peer,), device_id_type=MESH
        )
        copy.start()
        return copy

    mine = pltpu.make_async_copy(region, table.at[pl.ds(me, 1)], own.at[0])
    mine.start()
    first = [
        remote(region, table.at[pl.ds(me, 1)], g1_s.at[k], g1_r.at[k], peer) for k, peer in enumerate(peers1)
    ]
    halo = [
        remote(packed.at[:, pl.ds(0, 128)], hc.at[0], cf_s.at[0], cf_r.at[0], right),
        remote(packed.at[:, pl.ds(0, 128)], hc.at[1], cf_s.at[1], cf_r.at[1], left),
        remote(xm.at[3], hx.at[0], px_s.at[0], px_r.at[0], right),
        remote(xm.at[0], hx.at[1], px_s.at[1], px_r.at[1], left),
    ]
    mine.wait()
    for copy in first:
        copy.wait()
    block = table.at[pl.ds(group * 16, 16)]
    second = [remote(block, block, g2_s.at[k], g2_r.at[k], peer) for k, peer in enumerate(peers2)]
    for copy in second:
        copy.wait()
    for copy in halo:
        copy.wait()


def top_blocks(me, offset_t, top_c):
    bases = (0, 256, 384, 448)
    lane = iota((8, 480), 1)
    offsets = offset_t[...].astype(F32)
    picks = []
    for h in range(4):
        chosen = jnp.sum(jnp.where(lane == bases[h] + (me >> h), offsets, 0.0), 1, keepdims=True)
        picks.append((iota((8, 160), 1).astype(F32) == chosen).astype(F32))
    pick = jnp.concatenate(picks, 0).astype(BF16)
    hi, lo = split(top_c[...].reshape(1024, 160))
    return dot(hi, pick, NT) + dot(lo, pick, NT)


def top_expand(me, table, partner_t, count, blocks, paths, path_ref):
    both, two, three, _ = paths
    bases = (0, 256, 384, 448)
    lane = iota((8, 480), 1)
    slot = iota((8, 256), 0)
    partners = partner_t[...].astype(F32)
    node = iota((8, 256), 1).astype(F32)
    picks = []
    for h in range(4):
        row = bases[h] + (me >> h)
        chosen = jnp.sum(jnp.where(lane == row, partners, 0.0), 1, keepdims=True) - bases[h]
        live = slot < count[row]
        for t in range(2**h):
            picks.append(jnp.where(live & (node == chosen * 2**h + t), 1.0, 0.0))
    pick = jnp.concatenate(picks, 0).astype(BF16)
    hi, lo = split(table)
    picked = dot(pick, hi) + dot(pick, lo)
    stacks = (None, both, two, three)
    first = 0
    nodes = [[], []]
    for h in range(4):
        merged = []
        for rhs in range(2):
            merged.append(
                jnp.concatenate(
                    [
                        picked[first + 8 * t : first + 8 * t + 8, rhs * 32 : rhs * 32 + 32]
                        for t in range(2**h)
                    ],
                    1,
                )
            )
        merged = jnp.concatenate(merged, 0)
        if h > 0:
            merged = dot3(merged, stacks[h])
        nodes[0].append(merged[0:8])
        nodes[1].append(merged[8:16])
        first += 8 * 2**h
    local = []
    for rhs in range(2):
        across = jnp.concatenate(nodes[rhs], 0).T
        total = jnp.zeros((32, 32), F32)
        for a in range(32):
            total = total + blocks[32 * a : 32 * a + 32] * across[a : a + 1]
        total = total.T
        local.append([jnp.sum(total[8 * h : 8 * h + 8], 0, keepdims=True) for h in range(4)])
    path_ref[0:64, 0:32] = both
    path_ref[64:192, 0:32] = two
    path_ref[192:448, 0:32] = three
    expansion = jnp.concatenate([local[0][0], local[1][0]] * 4, 0)
    starts = (0, 0, 64, 192)
    for h in range(1, 4):
        here = jnp.concatenate([local[0][h], local[1][h]] * 4, 0)
        begin = pl.multiple_of(starts[h] + (me & (2**h - 1)) * 32, 32)
        path = path_ref[pl.ds(begin, 32), :][:, 0:32]
        expansion = expansion + dot3(here, path, NT)
    return expansion[0:2]


def descend(expansion, v_ref, w_ref, paths):
    _, _, three, four = paths
    wide = dot3(jnp.concatenate([expansion] * 4, 0), four, NT)[0:2]
    for a in range(16):
        w_ref[pl.ds(a, 2, stride=16), 0:32] = wide[:, 32 * a : 32 * a + 32]
    wide = dot3(w_ref[:, 0:32], four, NT)
    for rhs in range(2):
        for b in range(16):
            v_ref[pl.ds(2 * b + rhs, 16, stride=32), 0:32] = wide[
                16 * rhs : 16 * rhs + 16, 32 * b : 32 * b + 32
            ]
    merge = jnp.concatenate(
        [
            three[(c * 4 + i) * 32 : (c * 4 + i) * 32 + 32]
            for i in (3, 2, 1, 0)
            for c in (1, 0)
        ],
        0,
    )
    return dot3(v_ref[:, 0:32], merge, NT)


def offset_number(a, b):
    if max(abs(a), abs(b)) < 2 or max(abs(a), abs(b)) > 3:
        return None
    number = 0
    for x in range(-3, 4):
        for y in range(-3, 4):
            if (x, y) == (a, b):
                return number
            if max(abs(x), abs(y)) >= 2:
                number += 1


BETAS = (-2, -1, 0, 1, 2, 3, 4, -3)
ROW_GROUPS = ((1, 2, 0, 3), (-3, -2, 5, 6, -1, 4))


def far_weights(coupling, window, w_hi, w_lo):
    window[...] = jnp.zeros_like(window)
    for at, beta in enumerate(BETAS):
        for a in range(-3, 4):
            for side in range(2):
                number = offset_number(a, beta - 1 + side)
                if number is not None:
                    block = coupling[number]
                    start = (a + 6) * 64 + side * 32
                    window[0, at, :, start : start + 32] = block
                    window[1, at, :, start + 64 : start + 96] = block
    row = 0
    for shift in range(4):
        for i in ROW_GROUPS[0] + ROW_GROUPS[1]:
            for c in range(2):
                start = (i + 3) * 64
                odd = (start // 64) % 2
                part = window[odd, 2 * shift + c, :, start + 64 * odd : start + 64 * odd + 256]
                hi, lo = split(part)
                w_hi[row : row + 32] = hi
                w_lo[row : row + 32] = lo
                row += 32


def far_field(coef, w_hi, w_lo, far):
    chunk = 128
    lane = iota((chunk, 640), 1)
    even = (lane & 32) == 0
    for m in range(512 // chunk):
        at = 8 + m * chunk
        views = [coef[pl.ds(at + 2 * d, chunk)] for d in (-1, 0, 1)]
        views.append(jnp.where(even, coef[pl.ds(at + 4, chunk)], coef[pl.ds(at - 4, chunk)]))
        parts = [split(view) for view in views]
        hi = jnp.concatenate([part[0] for part in parts], 1)
        lo = jnp.concatenate([part[1] for part in parts], 1)
        far[pl.ds(m * chunk, chunk)] = dot(hi, w_hi[...]) + dot(lo, w_hi[...]) + dot(hi, w_lo[...])


def kernel_down(
    n, xm, hx, packed, hc, table, mcol, bt, near, transfer, coupling, top_c, partner_t, offset_t, count, out,
    taps, coef, window, w_hi, w_lo, far, v_ref, w_ref, path_ref, weight, os, sem
):
    me = lax.axis_index("region")
    is_first = jnp.where(me > 0, 1.0, 0.0)
    is_last = jnp.where(me < n - 1, 1.0, 0.0)
    paths = tree_paths(transfer)
    blocks = top_blocks(me, offset_t, top_c)
    expansion = top_expand(me, table.reshape(256, 128)[...], partner_t, count, blocks, paths, path_ref)
    leaf = descend(expansion, v_ref, w_ref, paths)
    far_weights(coupling, window, w_hi, w_lo)
    hx0 = [hx[0, c] * is_first.astype(BF16) for c in range(2)]
    hx1 = [hx[1, c] * is_last.astype(BF16) for c in range(2)]
    zero8 = jnp.zeros((8, 640), F32)
    coef[0:8] = zero8
    coef[520:528] = zero8
    coef[8:520, 0:256] = packed[...]
    coef[8:520, 256:384] = hc[0] * is_first
    coef[8:520, 384:512] = hc[1] * is_last
    basis = bt[...]
    for k, rows in enumerate((hx0, hx1)):
        for c in range(2):
            start = 512 + 64 * k + 32 * c
            coef[8:520, start : start + 32] = dot(rows[c], basis, NT)
    far_field(coef, w_hi, w_lo, far)
    leaf = leaf + far[...]
    hi, lo = split(leaf)
    for r in range(6):
        rows = hx0 if r == 0 else hx1 if r == 5 else [xm[r - 1, 0], xm[r - 1, 1]]
        taps[r, 0, 16:528] = rows[0]
        taps[r, 1, 16:528] = rows[1]
        taps[r, 0, 528:544] = jnp.zeros((16, 256), BF16)
        taps[r, 1, 0:16] = jnp.zeros((16, 256), BF16)
        taps[r, 2, 16:528] = taps[r, 0, 18:530]
        taps[r, 3, 16:528] = taps[r, 1, 14:526]
    order = ((3, 0, 1), (0, 1, 2))
    weight[...] = jnp.zeros_like(weight)
    for i2 in range(2):
        for c in range(2):
            start = (1 - i2) * 64 + (1 - c) * 32
            weight[i2, c, pl.ds(start, 32)] = basis
            weight[i2, c, pl.ds(128 + start, 32)] = basis
    copies = []
    chunk = 256
    for i in range(4):
        for c in range(2):
            half = 0 if i >= 2 else 128
            for m in range(512 // chunk):
                rows = pl.ds(16 + m * chunk, chunk)
                parts = [taps[i + a, order[c][b], rows] for a in range(3) for b in range(3)]
                acc = dot(jnp.concatenate(parts, 1), near[...])
                tail = slice(m * chunk, (m + 1) * chunk)
                exps = jnp.concatenate([hi[tail, half : half + 128], lo[tail, half : half + 128]], 1)
                acc = acc + dot(exps, weight[i % 2, c])
                col = mcol[i, c, pl.ds(m * chunk, chunk)].astype(F32)
                for lt in range(2):
                    os.at[i, c, lt].reshape(512, 128)[pl.ds(m * chunk, chunk)] = (
                        acc[:, lt * 128 : lt * 128 + 128] * col
                    )
            for lt in range(2):
                copy = pltpu.make_async_copy(
                    os.at[i, c, lt], out.at[i, :, c, :, pl.ds(lt * 128, 128)], sem.at[i, c, lt]
                )
                copy.start()
                copies.append(copy)
    for copy in copies:
        copy.wait()


def body(n, pixels, valid, basis, near, transfer, coupling, top_c, partner, offset, count):
    x = pixels.reshape(4, 256, 2, 2, 256)
    bt = basis.T
    vmem = pl.BlockSpec(memory_space=pltpu.VMEM)
    anywhere = pl.BlockSpec(memory_space=pl.ANY)
    sds = jax.ShapeDtypeStruct
    dma = pltpu.SemaphoreType.DMA
    xm, mcol, packed, region = pl.pallas_call(
        kernel_up,
        out_shape=(sds((4, 2, 512, 256), BF16), sds((4, 2, 512, 128), BF16), sds((512, 256), F32), sds((1, 1, 128), F32)),
        in_specs=[anywhere, vmem, vmem, vmem],
        out_specs=(vmem, vmem, vmem, vmem),
        scratch_shapes=[
            pltpu.VMEM((4, 2, 2, 256, 2, 128), BF16),
            pltpu.VMEM((256, 2048), BF16),
            pltpu.VMEM((512, 128), F32),
            pltpu.VMEM((32, 128), F32),
            dma((4, 2, 2)),
        ],
        compiler_params=pltpu.CompilerParams(vmem_limit_bytes=VMEM_LIMIT),
    )(x, valid, bt, transfer)
    hx, hc, table = pl.pallas_call(
        functools.partial(kernel_move, n),
        out_shape=(sds((2, 2, 512, 256), BF16), sds((2, 512, 128), F32), sds((n, 1, 128), F32)),
        in_specs=[anywhere] * 3,
        out_specs=(anywhere,) * 3,
        scratch_shapes=[dma((2,)), dma((2,)), dma((2,)), dma((2,)), dma((15,)), dma((15,)), dma((n // 16 - 1,)), dma((n // 16 - 1,)), dma((1,))],
        compiler_params=pltpu.CompilerParams(collective_id=0, has_side_effects=True),
    )(xm, packed, region)
    out = pl.pallas_call(
        functools.partial(kernel_down, n),
        out_shape=sds((4, 256, 2, 2, 256), F32),
        in_specs=[vmem] * 13 + [pl.BlockSpec(memory_space=pltpu.SMEM)],
        out_specs=anywhere,
        scratch_shapes=[
            pltpu.VMEM((6, 4, 544, 256), BF16),
            pltpu.VMEM((528, 640), F32),
            pltpu.VMEM((2, 8, 32, 1024), F32),
            pltpu.VMEM((2560, 256), BF16),
            pltpu.VMEM((2560, 256), BF16),
            pltpu.VMEM((512, 256), F32),
            pltpu.VMEM((512, 128), F32),
            pltpu.VMEM((32, 128), F32),
            pltpu.VMEM((448, 128), F32),
            pltpu.VMEM((2, 2, 256, 256), BF16),
            pltpu.VMEM((4, 2, 2, 256, 2, 128), F32),
            dma((4, 2, 2)),
        ],
        compiler_params=pltpu.CompilerParams(vmem_limit_bytes=VMEM_LIMIT),
    )(
        xm, hx, packed, hc, table, mcol, bt, near.reshape(2304, 256), transfer, coupling,
        jnp.transpose(top_c, (1, 2, 0)), partner.T, offset.T, count,
    )
    return out.reshape(4, 512, 2, 256)


def solution(mesh):
    n = mesh.shape["region"]
    in_specs = (P("region", None, None, None), P("region", None)) + (P(),) * 8
    out_specs = P("region", None, None, None)
    return jax.shard_map(functools.partial(body, n), mesh=mesh, in_specs=in_specs, out_specs=out_specs, check_vma=False)
```

```python
import functools

import jax
import jax.numpy as jnp
from jax import lax
from jax.experimental import pallas as pl
from jax.experimental.pallas import tpu as pltpu
from jax.sharding import PartitionSpec as P

MESH = pl.DeviceIdType.MESH
F32 = jnp.float32
BF16 = jnp.bfloat16
NN = (((1,), (0,)), ((), ()))
NT = (((1,), (1,)), ((), ()))
IN_ORDER = (1, 2, 0, 3)
VMEM_LIMIT = 56 << 20


def dot(a, b, dims=NN):
    return lax.dot_general(a, b, dims, preferred_element_type=F32)


def split(x):
    hi = x.astype(BF16)
    return hi, (x - hi.astype(F32)).astype(BF16)


def dot3(a, b, dims=NN):
    a_hi, a_lo = split(a)
    b_hi, b_lo = split(b)
    return dot(a_hi, b_hi, dims) + (dot(a_lo, b_hi, dims) + dot(a_hi, b_lo, dims))


def iota(shape, axis):
    return lax.broadcasted_iota(jnp.int32, shape, axis)


def local(src, dst, sem):
    copy = pltpu.make_async_copy(src, dst, sem)
    copy.start()
    return copy


def await_bytes(ref, sem):
    pltpu.make_async_copy(ref, ref, sem).wait()


def tree_paths(transfer):
    side0, side1 = transfer[0], transfer[1]
    both = jnp.concatenate([side0, side1], 0)
    lanes = jnp.concatenate([side0, side1], 1)
    pairs = dot3(both, lanes)
    two = jnp.concatenate([pairs[:, :32], pairs[:, 32:]], 0)
    three = dot3(two, lanes)
    three = jnp.concatenate([three[:, :32], three[:, 32:]], 0)
    two_lanes = jnp.concatenate([two[32 * s : 32 * s + 32] for s in range(4)], 1)
    four = dot3(two, two_lanes)
    four = jnp.concatenate([four[:, 32 * s : 32 * s + 32] for s in range(4)], 0)
    return both, two, three, four


def mask_rows(valid):
    values = valid.astype(F32).astype(BF16)
    values = jnp.concatenate([values, values], 0)
    lane = iota((512, 1024), 1)
    leaf = (lane & 510) + (lane >> 9)
    pick = (iota((512, 1024), 0) == leaf).astype(F32).astype(BF16)
    return dot(values, pick)


def column(row):
    return jnp.concatenate(
        [jnp.broadcast_to(row[:, 128 * b : 128 * b + 128], (128, 128)).T for b in range(4)], 0
    )


def climb(packed, v_ref, w_ref, paths):
    _, _, three, four = paths
    merge = jnp.concatenate(
        [three[(c * 4 + i) * 32 : (c * 4 + i) * 32 + 32] for i in IN_ORDER for c in range(2)], 0
    )
    v_ref[:, 0:32] = dot3(packed, merge)
    rows = []
    for rhs in range(2):
        rows.append(
            jnp.concatenate(
                [v_ref[pl.ds(2 * b + rhs, 16, stride=32), :][:, 0:32] for b in range(16)], 1
            )
        )
    w_ref[:, 0:32] = dot3(jnp.concatenate(rows, 0), four)
    last = jnp.concatenate([w_ref[pl.ds(a, 2, stride=16), :][:, 0:32] for a in range(16)], 1)
    return dot3(jnp.concatenate([last, last, last, last], 0), four)[0:2]


def top_blocks(me, offset_t, top_c):
    bases = (0, 256, 384, 448)
    lane = iota((8, 480), 1)
    offsets = offset_t[...].astype(F32)
    picks = []
    for h in range(4):
        chosen = jnp.sum(jnp.where(lane == bases[h] + (me >> h), offsets, 0.0), 1, keepdims=True)
        picks.append((iota((8, 160), 1).astype(F32) == chosen).astype(F32))
    pick = jnp.concatenate(picks, 0).astype(BF16)
    hi, lo = split(top_c[...].reshape(1024, 160))
    return dot(hi, pick, NT) + dot(lo, pick, NT)


def top_expand(me, table, partner_t, count, blocks, paths, path_ref):
    both, two, three, _ = paths
    bases = (0, 256, 384, 448)
    lane = iota((8, 480), 1)
    slot = iota((8, 256), 0)
    partners = partner_t[...].astype(F32)
    node = iota((8, 256), 1).astype(F32)
    picks = []
    for h in range(4):
        row = bases[h] + (me >> h)
        chosen = jnp.sum(jnp.where(lane == row, partners, 0.0), 1, keepdims=True) - bases[h]
        live = slot < count[row]
        for t in range(2**h):
            picks.append(jnp.where(live & (node == chosen * 2**h + t), 1.0, 0.0))
    pick = jnp.concatenate(picks, 0).astype(BF16)
    hi, lo = split(table)
    picked = dot(pick, hi) + dot(pick, lo)
    stacks = (None, both, two, three)
    first = 0
    nodes = [[], []]
    for h in range(4):
        merged = []
        for rhs in range(2):
            merged.append(
                jnp.concatenate(
                    [
                        picked[first + 8 * t : first + 8 * t + 8, rhs * 32 : rhs * 32 + 32]
                        for t in range(2**h)
                    ],
                    1,
                )
            )
        merged = jnp.concatenate(merged, 0)
        if h > 0:
            merged = dot3(merged, stacks[h])
        nodes[0].append(merged[0:8])
        nodes[1].append(merged[8:16])
        first += 8 * 2**h
    local = []
    for rhs in range(2):
        across = jnp.concatenate(nodes[rhs], 0).T
        total = jnp.zeros((32, 32), F32)
        for a in range(32):
            total = total + blocks[32 * a : 32 * a + 32] * across[a : a + 1]
        total = total.T
        local.append([jnp.sum(total[8 * h : 8 * h + 8], 0, keepdims=True) for h in range(4)])
    path_ref[0:64, 0:32] = both
    path_ref[64:192, 0:32] = two
    path_ref[192:448, 0:32] = three
    expansion = jnp.concatenate([local[0][0], local[1][0]] * 4, 0)
    starts = (0, 0, 64, 192)
    for h in range(1, 4):
        here = jnp.concatenate([local[0][h], local[1][h]] * 4, 0)
        begin = pl.multiple_of(starts[h] + (me & (2**h - 1)) * 32, 32)
        path = path_ref[pl.ds(begin, 32), :][:, 0:32]
        expansion = expansion + dot3(here, path, NT)
    return expansion[0:2]


def descend(expansion, v_ref, w_ref, paths):
    _, _, three, four = paths
    wide = dot3(jnp.concatenate([expansion] * 4, 0), four, NT)[0:2]
    for a in range(16):
        w_ref[pl.ds(a, 2, stride=16), 0:32] = wide[:, 32 * a : 32 * a + 32]
    wide = dot3(w_ref[:, 0:32], four, NT)
    for rhs in range(2):
        for b in range(16):
            v_ref[pl.ds(2 * b + rhs, 16, stride=32), 0:32] = wide[
                16 * rhs : 16 * rhs + 16, 32 * b : 32 * b + 32
            ]
    merge = jnp.concatenate(
        [
            three[(c * 4 + i) * 32 : (c * 4 + i) * 32 + 32]
            for i in (3, 2, 1, 0)
            for c in (1, 0)
        ],
        0,
    )
    return dot3(v_ref[:, 0:32], merge, NT)


OFFSETS = [(a, b) for a in range(-3, 4) for b in range(-3, 4) if max(abs(a), abs(b)) >= 2]
BETAS = (-2, -1, 0, 1, 2, 3, 4, -3)
ROW_GROUPS = ((1, 2, 0, 3), (-3, -2, 5, 6, -1, 4))


def far_weights(coupling, blocks, window, w_hi, w_lo):
    for k in range(32):
        blocks[pl.ds(40 * k, 40), 0:32] = coupling[k].T
    window[...] = jnp.zeros_like(window)
    for number, (a, b) in enumerate(OFFSETS):
        block = blocks[pl.ds(number, 32, stride=40), :][:, 0:32]
        for at, beta in enumerate(BETAS):
            for side in range(2):
                if beta - 1 + side == b:
                    start = (a + 6) * 64 + side * 32
                    window[0, at, :, start : start + 32] = block
                    window[1, at, :, start + 64 : start + 96] = block
    row = 0
    for group in ROW_GROUPS:
        for shift in range(4):
            for i in group:
                for c in range(2):
                    start = (i + 3) * 64
                    odd = (start // 64) % 2
                    part = window[odd, 2 * shift + c, :, start + 64 * odd : start + 64 * odd + 256]
                    hi, lo = split(part)
                    w_hi[row : row + 32] = hi
                    w_lo[row : row + 32] = lo
                    row += 32


def far_field(coef, first, w_hi, w_lo, far):
    chunk = 128
    lanes = coef.shape[1]
    even = (iota((chunk, lanes), 1) & 32) == 0
    weights = pl.ds(first, 4 * lanes)
    for m in range(512 // chunk):
        at = 8 + m * chunk
        views = [coef[pl.ds(at + 2 * d, chunk)] for d in (-1, 0, 1)]
        views.append(jnp.where(even, coef[pl.ds(at + 4, chunk)], coef[pl.ds(at - 4, chunk)]))
        parts = [split(view) for view in views]
        hi = jnp.concatenate([part[0] for part in parts], 1)
        lo = jnp.concatenate([part[1] for part in parts], 1)
        total = dot(hi, w_hi[weights]) + dot(lo, w_hi[weights]) + dot(hi, w_lo[weights])
        rows = pl.ds(m * chunk, chunk)
        far[rows] = total if first == 0 else far[rows] + total


ORDER = ((3, 0, 1), (0, 1, 2))
CHUNK = 256


def shifted(taps, r):
    taps[r, 0, 528:544] = jnp.zeros((16, 256), BF16)
    taps[r, 1, 0:16] = jnp.zeros((16, 256), BF16)
    taps[r, 2, 16:528] = taps[r, 0, 18:530]
    taps[r, 3, 16:528] = taps[r, 1, 14:526]


def near_rows(taps, near, acc, i, rows, add):
    first, count = rows[0], len(rows)
    for c in range(2):
        for m in range(512 // CHUNK):
            span = pl.ds(16 + m * CHUNK, CHUNK)
            parts = [taps[i + a, ORDER[c][b], span] for a in rows for b in range(3)]
            total = dot(jnp.concatenate(parts, 1), near[pl.ds(768 * first, 768 * count)])
            out = pl.ds(m * CHUNK, CHUNK)
            acc[i, c, out] = acc[i, c, out] + total if add else total


def kernel_main(
    n, x, near_any, coupling_any, top_any, valid, bt, transfer, partner_t, offset_t, count, acc_out, exp_out, mcol_out,
    xs, near, coupling, top_c, mcol, taps, basis, packed, coef, coef_halo, hc, table, blocks, window, w_hi, w_lo, far,
    acc, exps, v_ref, w_ref, path_ref, x_sem, w_sem, px_s, px_r, cf_s, cf_r, g_s, g_r, o_sem
):
    me = lax.axis_index("region")
    right, left = lax.rem(me + 1, n), lax.rem(me + n - 1, n)
    group = me // 16
    spot = lax.rem(me, 16)
    groups = n // 16
    barrier = pltpu.get_barrier_semaphore()
    peers1 = [group * 16 + lax.rem(spot + k, 16) for k in range(1, 16)]
    peers2 = [lax.rem(group + k, groups) * 16 + spot for k in range(1, groups)]

    def remote(src, dst, send, recv, peer):
        copy = pltpu.make_async_remote_copy(
            src_ref=src, dst_ref=dst, send_sem=send, recv_sem=recv, device_id=(peer,), device_id_type=MESH
        )
        copy.start()
        return copy

    for peer in [left, right] + peers1 + peers2:
        pl.semaphore_signal(barrier, inc=1, device_id=(peer,), device_id_type=MESH)
    for i in (0, 3, 1, 2):
        for c in range(2):
            for lt in range(2):
                local(x.at[i, :, c, :, pl.ds(lt * 128, 128)], xs.at[i, c, lt], x_sem.at[i])
    near_load = local(near_any, near, w_sem.at[0])
    coupling_load = local(coupling_any, coupling, w_sem.at[1])
    top_load = local(top_any, top_c, w_sem.at[2])

    basis[...] = jnp.zeros_like(basis)
    for at, i in enumerate(IN_ORDER):
        for c in range(2):
            basis[pl.ds(at * 64 + c * 32, 32), pl.ds((i * 2 + c) * 256, 256)] = bt[...]
    paths = tree_paths(transfer)
    rows = mask_rows(valid[...])
    for i in (0, 3, 1, 2):
        await_bytes(xs.at[i], x_sem.at[i])
        for c in range(2):
            col = column(rows[i : i + 1, c * 512 : c * 512 + 512]).astype(BF16)
            mcol[i, c] = col
            for lt in range(2):
                part = xs.at[i, c, lt].reshape(512, 128)[...]
                taps[i + 1, c, 16:528, lt * 128 : lt * 128 + 128] = part * col
    mcol_copy = local(mcol, mcol_out, o_sem.at[0])
    pixels = jnp.concatenate([taps[i + 1, c, 16:528] for i in range(4) for c in range(2)], 1)
    packed[...] = dot(pixels, basis[...], NT)
    top = climb(packed[...], v_ref, w_ref, paths)
    table[pl.ds(me, 1)] = jnp.concatenate([top[0:1], top[1:2], jnp.zeros((1, 64), F32)], 1).reshape(1, 1, 128)

    pl.semaphore_wait(barrier, 2 + 15 + groups - 1)
    mine = table.at[pl.ds(me, 1)]
    for peer in peers1:
        remote(mine, mine, g_s.at[0], g_r.at[0], peer)
    sent = packed.at[:, pl.ds(0, 128)]
    coef_copies = [
        remote(sent, hc.at[0], cf_s.at[0], cf_r.at[0], right),
        remote(sent, hc.at[1], cf_s.at[1], cf_r.at[1], left),
    ]
    inside = pl.ds(16, 512)
    pixel_copies = [
        remote(taps.at[4, pl.ds(0, 2), inside], taps.at[0, pl.ds(0, 2), inside], px_s.at[0], px_r.at[0], right),
        remote(taps.at[1, pl.ds(0, 2), inside], taps.at[5, pl.ds(0, 2), inside], px_s.at[1], px_r.at[1], left),
    ]

    for r in range(1, 5):
        shifted(taps, r)
    near_load.wait()
    near_rows(taps, near, acc, 1, (0, 1, 2), False)
    near_rows(taps, near, acc, 2, (0, 1, 2), False)

    await_bytes(table.at[pl.ds(0, 15)], g_s.at[0])
    await_bytes(table.at[pl.ds(0, 15)], g_r.at[0])
    block = table.at[pl.ds(group * 16, 16)]
    for peer in peers2:
        remote(block, block, g_s.at[1], g_r.at[1], peer)

    inner_copy = local(acc.at[pl.ds(1, 2)], acc_out.at[pl.ds(1, 2)], o_sem.at[1])
    coupling_load.wait()
    far_weights(coupling, blocks, window, w_hi, w_lo)
    top_load.wait()
    slots = top_blocks(me, offset_t, top_c)
    coef[0:8] = jnp.zeros((8, 256), F32)
    coef[520:528] = jnp.zeros((8, 256), F32)
    coef[8:520] = packed[...]
    far_field(coef, 0, w_hi, w_lo, far)
    near_rows(taps, near, acc, 0, (1, 2), False)
    near_rows(taps, near, acc, 3, (0, 1), False)

    for copy in pixel_copies:
        copy.wait()

    @pl.when(me == 0)
    def _():
        taps[0, 0:2, 16:528] = jnp.zeros((2, 512, 256), BF16)

    @pl.when(me == n - 1)
    def _():
        taps[5, 0:2, 16:528] = jnp.zeros((2, 512, 256), BF16)

    shifted(taps, 0)
    shifted(taps, 5)
    near_rows(taps, near, acc, 0, (0,), True)
    near_rows(taps, near, acc, 3, (2,), True)
    outer_copies = [local(acc.at[i], acc_out.at[i], o_sem.at[k]) for k, i in ((2, 0), (3, 3))]

    for copy in coef_copies:
        copy.wait()
    coef_halo[0:8] = jnp.zeros((8, 384), F32)
    coef_halo[520:528] = jnp.zeros((8, 384), F32)
    coef_halo[8:520, 0:128] = hc[0] * jnp.where(me > 0, 1.0, 0.0)
    coef_halo[8:520, 128:256] = hc[1] * jnp.where(me < n - 1, 1.0, 0.0)
    for k, r in enumerate((0, 5)):
        for c in range(2):
            start = 256 + 64 * k + 32 * c
            coef_halo[8:520, start : start + 32] = dot(taps[r, c, 16:528], bt[...], NT)
    far_field(coef_halo, 1024, w_hi, w_lo, far)

    await_bytes(table.at[pl.ds(0, n - 16)], g_s.at[1])
    await_bytes(table.at[pl.ds(0, n - 16)], g_r.at[1])
    expansion = top_expand(me, table.reshape(n, 128)[...], partner_t, count, slots, paths, path_ref)
    leaf = descend(expansion, v_ref, w_ref, paths) + far[...]
    hi, lo = split(leaf)
    for half in range(2):
        exps[half, :, 0:128] = hi[:, half * 128 : half * 128 + 128]
        exps[half, :, 128:256] = lo[:, half * 128 : half * 128 + 128]
    exp_copy = local(exps, exp_out, o_sem.at[4])
    for copy in [mcol_copy, inner_copy] + outer_copies + [exp_copy]:
        copy.wait()


def kernel_out(acc_any, exps, mcol_any, bt, out, acc, mcol, weight, os, in_sem, out_sem):
    loads = [
        (local(acc_any.at[i, c], acc.at[i, c], in_sem.at[i, c]), local(mcol_any.at[i, c], mcol.at[i, c], in_sem.at[4 + i, c]))
        for i in range(4)
        for c in range(2)
    ]
    weight[...] = jnp.zeros_like(weight)
    for i2 in range(2):
        for c in range(2):
            start = (1 - i2) * 64 + (1 - c) * 32
            weight[i2, c, pl.ds(start, 32)] = bt[...]
            weight[i2, c, pl.ds(128 + start, 32)] = bt[...]
    for i in range(4):
        for c in range(2):
            for copy in loads[i * 2 + c]:
                copy.wait()
            total = acc[i, c] + dot(exps[1 - i // 2], weight[i % 2, c])
            col = mcol[i, c].astype(F32)
            for lt in range(2):
                os.at[i, c, lt].reshape(512, 128)[...] = total[:, lt * 128 : lt * 128 + 128] * col
                local(os.at[i, c, lt], out.at[i, :, c, :, pl.ds(lt * 128, 128)], out_sem.at[0])
    await_bytes(os, out_sem.at[0])


def body(n, pixels, valid, basis, near, transfer, coupling, top_c, partner, offset, count):
    x = pixels.reshape(4, 256, 2, 2, 256)
    bt = basis.T
    vmem = pl.BlockSpec(memory_space=pltpu.VMEM)
    anywhere = pl.BlockSpec(memory_space=pl.ANY)
    sds = jax.ShapeDtypeStruct
    dma = pltpu.SemaphoreType.DMA
    acc, exps, mcol = pl.pallas_call(
        functools.partial(kernel_main, n),
        out_shape=(sds((4, 2, 512, 256), F32), sds((2, 512, 256), BF16), sds((4, 2, 512, 128), BF16)),
        in_specs=[anywhere] * 4 + [vmem] * 5 + [pl.BlockSpec(memory_space=pltpu.SMEM)],
        out_specs=(anywhere,) * 3,
        scratch_shapes=[
            pltpu.VMEM((4, 2, 2, 256, 2, 128), BF16),
            pltpu.VMEM((2304, 256), BF16),
            pltpu.VMEM((32, 32, 40), F32),
            pltpu.VMEM((32, 32, 160), F32),
            pltpu.VMEM((4, 2, 512, 128), BF16),
            pltpu.VMEM((6, 4, 544, 256), BF16),
            pltpu.VMEM((256, 2048), BF16),
            pltpu.VMEM((512, 256), F32),
            pltpu.VMEM((528, 256), F32),
            pltpu.VMEM((528, 384), F32),
            pltpu.VMEM((2, 512, 128), F32),
            pltpu.VMEM((n, 1, 128), F32),
            pltpu.VMEM((1280, 128), F32),
            pltpu.VMEM((2, 8, 32, 1024), F32),
            pltpu.VMEM((2560, 256), BF16),
            pltpu.VMEM((2560, 256), BF16),
            pltpu.VMEM((512, 256), F32),
            pltpu.VMEM((4, 2, 512, 256), F32),
            pltpu.VMEM((2, 512, 256), BF16),
            pltpu.VMEM((512, 128), F32),
            pltpu.VMEM((32, 128), F32),
            pltpu.VMEM((448, 128), F32),
            dma((4,)),
            dma((3,)),
            dma((2,)),
            dma((2,)),
            dma((2,)),
            dma((2,)),
            dma((2,)),
            dma((2,)),
            dma((5,)),
        ],
        compiler_params=pltpu.CompilerParams(collective_id=0, has_side_effects=True, vmem_limit_bytes=VMEM_LIMIT),
    )(
        x, near.reshape(2304, 256), jnp.transpose(coupling, (1, 2, 0)), jnp.transpose(top_c, (1, 2, 0)),
        valid, bt, transfer, partner.T, offset.T, count,
    )
    out = pl.pallas_call(
        kernel_out,
        out_shape=sds((4, 256, 2, 2, 256), F32),
        in_specs=[anywhere, vmem, anywhere, vmem],
        out_specs=anywhere,
        scratch_shapes=[
            pltpu.VMEM((4, 2, 512, 256), F32),
            pltpu.VMEM((4, 2, 512, 128), BF16),
            pltpu.VMEM((2, 2, 256, 256), BF16),
            pltpu.VMEM((4, 2, 2, 256, 2, 128), F32),
            dma((8, 2)),
            dma((1,)),
        ],
        compiler_params=pltpu.CompilerParams(vmem_limit_bytes=VMEM_LIMIT),
    )(acc, exps, mcol, bt)
    return out.reshape(4, 512, 2, 256)


def solution(mesh):
    n = mesh.shape["region"]
    in_specs = (P("region", None, None, None), P("region", None)) + (P(),) * 8
    out_specs = P("region", None, None, None)
    return jax.shard_map(functools.partial(body, n), mesh=mesh, in_specs=in_specs, out_specs=out_specs, check_vma=False)
```

```python
import functools

import jax
import jax.numpy as jnp
from jax import lax
from jax.experimental import pallas as pl
from jax.experimental.pallas import tpu as pltpu
from jax.sharding import PartitionSpec as P

MESH = pl.DeviceIdType.MESH
F32 = jnp.float32
BF16 = jnp.bfloat16
NN = (((1,), (0,)), ((), ()))
NT = (((1,), (1,)), ((), ()))
IN_ORDER = (1, 2, 0, 3)
VMEM_LIMIT = 56 << 20


def dot(a, b, dims=NN):
    return lax.dot_general(a, b, dims, preferred_element_type=F32)


def split(x):
    hi = x.astype(BF16)
    return hi, (x - hi.astype(F32)).astype(BF16)


def dot3(a, b, dims=NN):
    a_hi, a_lo = split(a)
    b_hi, b_lo = split(b)
    return dot(a_hi, b_hi, dims) + (dot(a_lo, b_hi, dims) + dot(a_hi, b_lo, dims))


def iota(shape, axis):
    return lax.broadcasted_iota(jnp.int32, shape, axis)


def local(src, dst, sem):
    copy = pltpu.make_async_copy(src, dst, sem)
    copy.start()
    return copy


def await_bytes(ref, sem):
    pltpu.make_async_copy(ref, ref, sem).wait()


def tree_paths(transfer):
    side0, side1 = transfer[0], transfer[1]
    both = jnp.concatenate([side0, side1], 0)
    lanes = jnp.concatenate([side0, side1], 1)
    pairs = dot3(both, lanes)
    two = jnp.concatenate([pairs[:, :32], pairs[:, 32:]], 0)
    three = dot3(two, lanes)
    three = jnp.concatenate([three[:, :32], three[:, 32:]], 0)
    two_lanes = jnp.concatenate([two[32 * s : 32 * s + 32] for s in range(4)], 1)
    four = dot3(two, two_lanes)
    four = jnp.concatenate([four[:, 32 * s : 32 * s + 32] for s in range(4)], 0)
    return both, two, three, four


def mask_rows(valid):
    values = valid.astype(F32).astype(BF16)
    values = jnp.concatenate([values, values], 0)
    lane = iota((512, 1024), 1)
    leaf = (lane & 510) + (lane >> 9)
    pick = (iota((512, 1024), 0) == leaf).astype(F32).astype(BF16)
    return dot(values, pick)


def column(row):
    return jnp.concatenate(
        [jnp.broadcast_to(row[:, 128 * b : 128 * b + 128], (128, 128)).T for b in range(4)], 0
    )


def climb(packed, v_ref, w_ref, paths):
    _, _, three, four = paths
    merge = jnp.concatenate(
        [three[(c * 4 + i) * 32 : (c * 4 + i) * 32 + 32] for i in IN_ORDER for c in range(2)], 0
    )
    v_ref[:, 0:32] = dot3(packed, merge)
    rows = []
    for rhs in range(2):
        rows.append(
            jnp.concatenate(
                [v_ref[pl.ds(2 * b + rhs, 16, stride=32), :][:, 0:32] for b in range(16)], 1
            )
        )
    w_ref[:, 0:32] = dot3(jnp.concatenate(rows, 0), four)
    last = jnp.concatenate([w_ref[pl.ds(a, 2, stride=16), :][:, 0:32] for a in range(16)], 1)
    return dot3(jnp.concatenate([last, last, last, last], 0), four)[0:2]


def top_blocks(me, offset_t, top_c):
    bases = (0, 256, 384, 448)
    lane = iota((8, 480), 1)
    offsets = offset_t[...].astype(F32)
    picks = []
    for h in range(4):
        chosen = jnp.sum(jnp.where(lane == bases[h] + (me >> h), offsets, 0.0), 1, keepdims=True)
        picks.append((iota((8, 160), 1).astype(F32) == chosen).astype(F32))
    pick = jnp.concatenate(picks, 0).astype(BF16)
    hi, lo = split(top_c[...].reshape(1024, 160))
    return dot(hi, pick, NT) + dot(lo, pick, NT)


def top_expand(me, table, partner_t, count, blocks, paths, path_ref):
    both, two, three, _ = paths
    bases = (0, 256, 384, 448)
    lane = iota((8, 480), 1)
    slot = iota((8, 256), 0)
    partners = partner_t[...].astype(F32)
    node = iota((8, 256), 1).astype(F32)
    picks = []
    for h in range(4):
        row = bases[h] + (me >> h)
        chosen = jnp.sum(jnp.where(lane == row, partners, 0.0), 1, keepdims=True) - bases[h]
        live = slot < count[row]
        for t in range(2**h):
            picks.append(jnp.where(live & (node == chosen * 2**h + t), 1.0, 0.0))
    pick = jnp.concatenate(picks, 0).astype(BF16)
    hi, lo = split(table)
    picked = dot(pick, hi) + dot(pick, lo)
    stacks = (None, both, two, three)
    first = 0
    nodes = [[], []]
    for h in range(4):
        merged = []
        for rhs in range(2):
            merged.append(
                jnp.concatenate(
                    [
                        picked[first + 8 * t : first + 8 * t + 8, rhs * 32 : rhs * 32 + 32]
                        for t in range(2**h)
                    ],
                    1,
                )
            )
        merged = jnp.concatenate(merged, 0)
        if h > 0:
            merged = dot3(merged, stacks[h])
        nodes[0].append(merged[0:8])
        nodes[1].append(merged[8:16])
        first += 8 * 2**h
    local = []
    for rhs in range(2):
        across = jnp.concatenate(nodes[rhs], 0).T
        total = jnp.zeros((32, 32), F32)
        for a in range(32):
            total = total + blocks[32 * a : 32 * a + 32] * across[a : a + 1]
        total = total.T
        local.append([jnp.sum(total[8 * h : 8 * h + 8], 0, keepdims=True) for h in range(4)])
    path_ref[0:64, 0:32] = both
    path_ref[64:192, 0:32] = two
    path_ref[192:448, 0:32] = three
    expansion = jnp.concatenate([local[0][0], local[1][0]] * 4, 0)
    starts = (0, 0, 64, 192)
    for h in range(1, 4):
        here = jnp.concatenate([local[0][h], local[1][h]] * 4, 0)
        begin = pl.multiple_of(starts[h] + (me & (2**h - 1)) * 32, 32)
        path = path_ref[pl.ds(begin, 32), :][:, 0:32]
        expansion = expansion + dot3(here, path, NT)
    return expansion[0:2]


def descend(expansion, v_ref, w_ref, paths):
    _, _, three, four = paths
    wide = dot3(jnp.concatenate([expansion] * 4, 0), four, NT)[0:2]
    for a in range(16):
        w_ref[pl.ds(a, 2, stride=16), 0:32] = wide[:, 32 * a : 32 * a + 32]
    wide = dot3(w_ref[:, 0:32], four, NT)
    for rhs in range(2):
        for b in range(16):
            v_ref[pl.ds(2 * b + rhs, 16, stride=32), 0:32] = wide[
                16 * rhs : 16 * rhs + 16, 32 * b : 32 * b + 32
            ]
    merge = jnp.concatenate(
        [
            three[(c * 4 + i) * 32 : (c * 4 + i) * 32 + 32]
            for i in (3, 2, 1, 0)
            for c in (1, 0)
        ],
        0,
    )
    return dot3(v_ref[:, 0:32], merge, NT)


OFFSETS = [(a, b) for a in range(-3, 4) for b in range(-3, 4) if max(abs(a), abs(b)) >= 2]
BETAS = (-2, -1, 0, 1, 2, 3, 4, -3)
ROW_GROUPS = ((1, 2, 0, 3), (-3, -2, 5, 6, -1, 4))


def far_weights(coupling, blocks, window, w_hi, w_lo):
    for k in range(32):
        blocks[pl.ds(40 * k, 40), 0:32] = coupling[k].T
    window[...] = jnp.zeros_like(window)
    for number, (a, b) in enumerate(OFFSETS):
        block = blocks[pl.ds(number, 32, stride=40), :][:, 0:32]
        for at, beta in enumerate(BETAS):
            for side in range(2):
                if beta - 1 + side == b:
                    start = (a + 6) * 64 + side * 32
                    window[0, at, :, start : start + 32] = block
                    window[1, at, :, start + 64 : start + 96] = block
    row = 0
    for group in ROW_GROUPS:
        for shift in range(4):
            for i in group:
                for c in range(2):
                    start = (i + 3) * 64
                    odd = (start // 64) % 2
                    part = window[odd, 2 * shift + c, :, start + 64 * odd : start + 64 * odd + 256]
                    hi, lo = split(part)
                    w_hi[row : row + 32] = hi
                    w_lo[row : row + 32] = lo
                    row += 32


def far_field(coef, first, w_hi, w_lo, far):
    chunk = 128
    lanes = coef.shape[1]
    even = (iota((chunk, lanes), 1) & 32) == 0
    weights = pl.ds(first, 4 * lanes)
    for m in range(512 // chunk):
        at = 8 + m * chunk
        views = [coef[pl.ds(at + 2 * d, chunk)] for d in (-1, 0, 1)]
        views.append(jnp.where(even, coef[pl.ds(at + 4, chunk)], coef[pl.ds(at - 4, chunk)]))
        parts = [split(view) for view in views]
        hi = jnp.concatenate([part[0] for part in parts], 1)
        lo = jnp.concatenate([part[1] for part in parts], 1)
        total = dot(hi, w_hi[weights]) + dot(lo, w_hi[weights]) + dot(hi, w_lo[weights])
        rows = pl.ds(m * chunk, chunk)
        far[rows] = total if first == 0 else far[rows] + total


ORDER = ((3, 0, 1), (0, 1, 2))
CHUNK = 256


def shifted(taps, r):
    taps[r, 0, 528:544] = jnp.zeros((16, 256), BF16)
    taps[r, 1, 0:16] = jnp.zeros((16, 256), BF16)
    taps[r, 2, 16:528] = taps[r, 0, 18:530]
    taps[r, 3, 16:528] = taps[r, 1, 14:526]


def near_rows(taps, near, acc, i, rows, add):
    first, count = rows[0], len(rows)
    for c in range(2):
        for m in range(512 // CHUNK):
            span = pl.ds(16 + m * CHUNK, CHUNK)
            parts = [taps[i + a - 1, ORDER[c][b], span] for a in rows for b in range(3)]
            total = dot(jnp.concatenate(parts, 1), near[pl.ds(768 * first, 768 * count)])
            out = pl.ds(m * CHUNK, CHUNK)
            acc[i, c, out] = acc[i, c, out] + total if add else total


def kernel_main(
    n, x, near_any, coupling_any, top_any, valid, bt, transfer, partner_t, offset_t, count, acc, exps, mcol, hx,
    xs, near, coupling, top_c, taps, basis, packed, inner_rows, outer, coef, coef_halo, hc, ho, table, blocks, window, w_hi, w_lo, far,
    v_ref, w_ref, path_ref, x_sem, w_sem, px_s, px_r, cf_s, cf_r, g_s, g_r
):
    me = lax.axis_index("region")
    right, left = lax.rem(me + 1, n), lax.rem(me + n - 1, n)
    group = me // 16
    spot = lax.rem(me, 16)
    groups = n // 16
    barrier = pltpu.get_barrier_semaphore()
    peers1 = [group * 16 + lax.rem(spot + k, 16) for k in range(1, 16)]
    peers2 = [lax.rem(group + k, groups) * 16 + spot for k in range(1, groups)]

    def remote(src, dst, send, recv, peer):
        copy = pltpu.make_async_remote_copy(
            src_ref=src, dst_ref=dst, send_sem=send, recv_sem=recv, device_id=(peer,), device_id_type=MESH
        )
        copy.start()
        return copy

    for i in (0, 3, 1, 2):
        for c in range(2):
            for lt in range(2):
                local(x.at[i, :, c, :, pl.ds(lt * 128, 128)], xs.at[i, c, lt], x_sem.at[i])
    near_load = local(near_any, near, w_sem.at[0])
    coupling_load = local(coupling_any, coupling, w_sem.at[1])
    top_load = local(top_any, top_c, w_sem.at[2])
    for peer in [left, right] + peers1 + peers2:
        pl.semaphore_signal(barrier, inc=1, device_id=(peer,), device_id_type=MESH)

    basis[...] = jnp.zeros_like(basis)
    for at, i in enumerate(IN_ORDER):
        for c in range(2):
            basis[pl.ds(at * 64 + c * 32, 32), pl.ds((i * 2 + c) * 256, 256)] = bt[...]
    paths = tree_paths(transfer)
    rows = mask_rows(valid[...])
    for i in (0, 3, 1, 2):
        await_bytes(xs.at[i], x_sem.at[i])
        for c in range(2):
            col = column(rows[i : i + 1, c * 512 : c * 512 + 512]).astype(BF16)
            mcol[i, c] = col
            for lt in range(2):
                part = xs.at[i, c, lt].reshape(512, 128)[...]
                taps[i, c, 16:528, lt * 128 : lt * 128 + 128] = part * col
    pixels = jnp.concatenate([taps[i, c, 16:528] for i in range(4) for c in range(2)], 1)
    packed[...] = dot(pixels, basis[...], NT)
    top = climb(packed[...], v_ref, w_ref, paths)
    table[pl.ds(me, 1)] = jnp.concatenate([top[0:1], top[1:2], jnp.zeros((1, 64), F32)], 1).reshape(1, 1, 128)

    pl.semaphore_wait(barrier, 2 + 15 + groups - 1)
    mine = table.at[pl.ds(me, 1)]
    for peer in peers1:
        remote(mine, mine, g_s.at[0], g_r.at[0], peer)
    for k in range(2):
        row = packed[:, 128 + 64 * k : 192 + 64 * k]
        outer[k] = jnp.concatenate([row[0:256], row[256:512]], 1)
    inner_rows[...] = packed[:, 0:128]
    coef_copies = [
        remote(inner_rows, hc.at[0], cf_s.at[0], cf_r.at[0], right),
        remote(inner_rows, hc.at[1], cf_s.at[1], cf_r.at[1], left),
        remote(outer.at[1], ho.at[0], cf_s.at[2], cf_r.at[2], right),
        remote(outer.at[0], ho.at[1], cf_s.at[3], cf_r.at[3], left),
    ]
    inside = pl.ds(16, 512)

    for r in range(4):
        shifted(taps, r)
    near_load.wait()
    near_rows(taps, near, acc, 1, (0, 1, 2), False)
    near_rows(taps, near, acc, 2, (0, 1, 2), False)
    near_rows(taps, near, acc, 0, (1, 2), False)
    near_rows(taps, near, acc, 3, (0, 1), False)
    coupling_load.wait()
    far_weights(coupling, blocks, window, w_hi, w_lo)
    coef[0:8] = jnp.zeros((8, 256), F32)
    coef[520:528] = jnp.zeros((8, 256), F32)
    coef[8:520] = packed[...]
    far_field(coef, 0, w_hi, w_lo, far)

    await_bytes(table.at[pl.ds(0, 15)], g_s.at[0])
    await_bytes(table.at[pl.ds(0, 15)], g_r.at[0])
    block = table.at[pl.ds(group * 16, 16)]
    for peer in peers2:
        remote(block, block, g_s.at[1], g_r.at[1], peer)
    pixel_copies = [
        remote(taps.at[3, 0, inside], hx.at[0, 0], px_s.at[0], px_r.at[0], right),
        remote(taps.at[0, 0, inside], hx.at[1, 0], px_s.at[1], px_r.at[1], left),
    ]
    pixel_copies += [
        remote(taps.at[3, 1, inside], hx.at[0, 1], px_s.at[2], px_r.at[2], right),
        remote(taps.at[0, 1, inside], hx.at[1, 1], px_s.at[3], px_r.at[3], left),
    ]

    top_load.wait()
    slots = top_blocks(me, offset_t, top_c)

    for copy in coef_copies:
        copy.wait()
    coef_halo[0:8] = jnp.zeros((8, 384), F32)
    coef_halo[520:528] = jnp.zeros((8, 384), F32)
    for k, inner in enumerate((jnp.where(me > 0, 1.0, 0.0), jnp.where(me < n - 1, 1.0, 0.0))):
        coef_halo[8:520, 128 * k : 128 * k + 128] = hc[k] * inner
        start = 256 + 64 * k
        row = ho[k] * inner
        coef_halo[8:264, start : start + 64] = row[:, 0:64]
        coef_halo[264:520, start : start + 64] = row[:, 64:128]
    far_field(coef_halo, 1024, w_hi, w_lo, far)

    await_bytes(table.at[pl.ds(0, n - 16)], g_s.at[1])
    await_bytes(table.at[pl.ds(0, n - 16)], g_r.at[1])
    expansion = top_expand(me, table.reshape(n, 128)[...], partner_t, count, slots, paths, path_ref)
    leaf = descend(expansion, v_ref, w_ref, paths) + far[...]
    hi, lo = split(leaf)
    for half in range(2):
        exps[half, :, 0:128] = hi[:, half * 128 : half * 128 + 128]
        exps[half, :, 128:256] = lo[:, half * 128 : half * 128 + 128]
    for copy in pixel_copies:
        copy.wait()


def kernel_out(n, acc, exps, mcol, hx, bt, near_any, out, weight, near, taps, os, in_sem, out_sem):
    near_loads = [local(near_any.at[pl.ds(1536 * k, 768)], near.at[k], in_sem.at[k]) for k in range(2)]
    me = lax.axis_index("region")
    weight[...] = jnp.zeros_like(weight)
    for i2 in range(2):
        for c in range(2):
            start = (1 - i2) * 64 + (1 - c) * 32
            weight[i2, c, pl.ds(start, 32)] = bt[...]
            weight[i2, c, pl.ds(128 + start, 32)] = bt[...]
    for i in (1, 2, 0, 3):
        edge = i // 3
        if i in (0, 3):
            inner = (jnp.where(me < n - 1, 1.0, 0.0) if edge else jnp.where(me > 0, 1.0, 0.0)).astype(BF16)
            for c in range(2):
                taps[edge, c, 16:528] = hx[edge, c] * inner
            shifted(taps, edge)
            near_loads[edge].wait()
        for c in range(2):
            total = acc[i, c] + dot(exps[1 - i // 2], weight[i % 2, c])
            if i in (0, 3):
                parts = [taps[edge, ORDER[c][b], 16:528] for b in range(3)]
                total = total + dot(jnp.concatenate(parts, 1), near[edge])
            col = mcol[i, c].astype(F32)
            for lt in range(2):
                os.at[i, c, lt].reshape(512, 128)[...] = total[:, lt * 128 : lt * 128 + 128] * col
                local(os.at[i, c, lt], out.at[i, :, c, :, pl.ds(lt * 128, 128)], out_sem.at[0])
    await_bytes(os, out_sem.at[0])


def body(n, pixels, valid, basis, near, transfer, coupling, top_c, partner, offset, count):
    x = pixels.reshape(4, 256, 2, 2, 256)
    bt = basis.T
    near = near.reshape(2304, 256)
    vmem = pl.BlockSpec(memory_space=pltpu.VMEM)
    anywhere = pl.BlockSpec(memory_space=pl.ANY)
    sds = jax.ShapeDtypeStruct
    dma = pltpu.SemaphoreType.DMA
    acc, exps, mcol, hx = pl.pallas_call(
        functools.partial(kernel_main, n),
        out_shape=(
            pltpu.VMEM((4, 2, 512, 256), F32), pltpu.VMEM((2, 512, 256), BF16), pltpu.VMEM((4, 2, 512, 128), BF16),
            pltpu.VMEM((2, 2, 512, 256), BF16),
        ),
        in_specs=[anywhere] * 4 + [vmem] * 5 + [pl.BlockSpec(memory_space=pltpu.SMEM)],
        out_specs=(vmem,) * 4,
        scratch_shapes=[
            pltpu.VMEM((4, 2, 2, 256, 2, 128), BF16),
            pltpu.VMEM((2304, 256), BF16),
            pltpu.VMEM((32, 32, 40), F32),
            pltpu.VMEM((32, 32, 160), F32),
            pltpu.VMEM((4, 4, 544, 256), BF16),
            pltpu.VMEM((256, 2048), BF16),
            pltpu.VMEM((512, 256), F32),
            pltpu.VMEM((512, 128), F32),
            pltpu.VMEM((2, 256, 128), F32),
            pltpu.VMEM((528, 256), F32),
            pltpu.VMEM((528, 384), F32),
            pltpu.VMEM((2, 512, 128), F32),
            pltpu.VMEM((2, 256, 128), F32),
            pltpu.VMEM((n, 1, 128), F32),
            pltpu.VMEM((1280, 128), F32),
            pltpu.VMEM((2, 8, 32, 1024), F32),
            pltpu.VMEM((2560, 256), BF16),
            pltpu.VMEM((2560, 256), BF16),
            pltpu.VMEM((512, 256), F32),
            pltpu.VMEM((512, 128), F32),
            pltpu.VMEM((32, 128), F32),
            pltpu.VMEM((448, 128), F32),
            dma((4,)),
            dma((3,)),
            dma((4,)),
            dma((4,)),
            dma((4,)),
            dma((4,)),
            dma((2,)),
            dma((2,)),
        ],
        compiler_params=pltpu.CompilerParams(collective_id=0, has_side_effects=True, vmem_limit_bytes=VMEM_LIMIT),
    )(
        x, near, jnp.transpose(coupling, (1, 2, 0)), jnp.transpose(top_c, (1, 2, 0)),
        valid, bt, transfer, partner.T, offset.T, count,
    )
    out = pl.pallas_call(
        functools.partial(kernel_out, n),
        out_shape=sds((4, 256, 2, 2, 256), F32),
        in_specs=[vmem] * 5 + [anywhere],
        out_specs=anywhere,
        scratch_shapes=[
            pltpu.VMEM((2, 2, 256, 256), BF16),
            pltpu.VMEM((2, 768, 256), BF16),
            pltpu.VMEM((2, 4, 544, 256), BF16),
            pltpu.VMEM((4, 2, 2, 256, 2, 128), F32),
            dma((2,)),
            dma((1,)),
        ],
        compiler_params=pltpu.CompilerParams(vmem_limit_bytes=24 << 20),
    )(*(pltpu.with_memory_space_constraint(a, pltpu.VMEM) for a in (acc, exps, mcol, hx)), bt, near)
    return out.reshape(4, 512, 2, 256)


def solution(mesh):
    n = mesh.shape["region"]
    in_specs = (P("region", None, None, None), P("region", None)) + (P(),) * 8
    out_specs = P("region", None, None, None)
    return jax.shard_map(functools.partial(body, n), mesh=mesh, in_specs=in_specs, out_specs=out_specs, check_vma=False)
```

```python
import functools

import jax
import jax.numpy as jnp
from jax import lax
from jax.experimental import pallas as pl
from jax.experimental.pallas import tpu as pltpu
from jax.sharding import PartitionSpec as P

MESH = pl.DeviceIdType.MESH
F32 = jnp.float32
BF16 = jnp.bfloat16
NN = (((1,), (0,)), ((), ()))
NT = (((1,), (1,)), ((), ()))
IN_ORDER = (1, 2, 0, 3)
VMEM_LIMIT = 56 << 20


def dot(a, b, dims=NN):
    return lax.dot_general(a, b, dims, preferred_element_type=F32)


def split(x):
    hi = x.astype(BF16)
    return hi, (x - hi.astype(F32)).astype(BF16)


def dot3(a, b, dims=NN):
    a_hi, a_lo = split(a)
    b_hi, b_lo = split(b)
    return dot(a_hi, b_hi, dims) + (dot(a_lo, b_hi, dims) + dot(a_hi, b_lo, dims))


def dot3_ready(a, b, dims=NN):
    a_hi, a_lo = split(a)
    return dot(a_hi, b[0], dims) + (dot(a_lo, b[0], dims) + dot(a_hi, b[1], dims))


def iota(shape, axis):
    return lax.broadcasted_iota(jnp.int32, shape, axis)


def local(src, dst, sem):
    copy = pltpu.make_async_copy(src, dst, sem)
    copy.start()
    return copy


def await_bytes(ref, sem):
    pltpu.make_async_copy(ref, ref, sem).wait()


def tree_paths(transfer):
    side0, side1 = transfer[0], transfer[1]
    both = jnp.concatenate([side0, side1], 0)
    lanes = jnp.concatenate([side0, side1], 1)
    pairs = dot3(both, lanes)
    two = jnp.concatenate([pairs[:, :32], pairs[:, 32:]], 0)
    three = dot3(two, lanes)
    three = jnp.concatenate([three[:, :32], three[:, 32:]], 0)
    two_lanes = jnp.concatenate([two[32 * s : 32 * s + 32] for s in range(4)], 1)
    four = dot3(two, two_lanes)
    four = jnp.concatenate([four[:, 32 * s : 32 * s + 32] for s in range(4)], 0)
    return both, two, three, four


def mask_rows(valid):
    values = valid.astype(F32).astype(BF16)
    values = jnp.concatenate([values, values], 0)
    lane = iota((512, 1024), 1)
    leaf = (lane & 510) + (lane >> 9)
    pick = (iota((512, 1024), 0) == leaf).astype(F32).astype(BF16)
    return dot(values, pick)


def column(row):
    return jnp.concatenate(
        [jnp.broadcast_to(row[:, 128 * b : 128 * b + 128], (128, 128)).T for b in range(4)], 0
    )


def leaf_paths(three, rows, sides):
    return jnp.concatenate(
        [three[(c * 4 + i) * 32 : (c * 4 + i) * 32 + 32] for i in rows for c in sides], 0
    )


def climb(packed, v_ref, w_ref, merge, four):
    v_ref[:, 0:32] = dot3_ready(packed, merge)
    rows = []
    for rhs in range(2):
        rows.append(
            jnp.concatenate(
                [v_ref[pl.ds(2 * b + rhs, 16, stride=32), :][:, 0:32] for b in range(16)], 1
            )
        )
    w_ref[:, 0:32] = dot3_ready(jnp.concatenate(rows, 0), four)
    last = jnp.concatenate([w_ref[pl.ds(a, 2, stride=16), :][:, 0:32] for a in range(16)], 1)
    return dot3_ready(jnp.concatenate([last, last, last, last], 0), four)[0:2]


def top_blocks(me, offset_t, top_c):
    bases = (0, 256, 384, 448)
    lane = iota((8, 480), 1)
    offsets = offset_t[...].astype(F32)
    picks = []
    for h in range(4):
        chosen = jnp.sum(jnp.where(lane == bases[h] + (me >> h), offsets, 0.0), 1, keepdims=True)
        picks.append((iota((8, 160), 1).astype(F32) == chosen).astype(F32))
    pick = jnp.concatenate(picks, 0).astype(BF16)
    hi, lo = split(top_c[...].reshape(1024, 160))
    return dot(hi, pick, NT) + dot(lo, pick, NT)


def top_picks(me, partner_t, count):
    bases = (0, 256, 384, 448)
    lane = iota((8, 480), 1)
    slot = iota((8, 256), 0)
    partners = partner_t[...].astype(F32)
    node = iota((8, 256), 1).astype(F32)
    picks = []
    for h in range(4):
        row = bases[h] + (me >> h)
        chosen = jnp.sum(jnp.where(lane == row, partners, 0.0), 1, keepdims=True) - bases[h]
        live = slot < count[row]
        for t in range(2**h):
            picks.append(jnp.where(live & (node == chosen * 2**h + t), 1.0, 0.0))
    return jnp.concatenate(picks, 0).astype(BF16)


def root_paths(me, paths, path_ref):
    both, two, three, four = paths
    path_ref[0:64, 0:32] = both
    path_ref[64:192, 0:32] = two
    path_ref[192:448, 0:32] = three
    starts = (0, 0, 64, 192)
    parts = [four]
    for h in range(1, 4):
        begin = pl.multiple_of(starts[h] + (me & (2**h - 1)) * 32, 32)
        parts.append(dot3(four, path_ref[pl.ds(begin, 32), :][:, 0:32]))
    return jnp.concatenate(parts, 1)


def top_expand(table, pick, blocks, stacks):
    hi, lo = split(table)
    picked = dot(pick, hi) + dot(pick, lo)
    first = 0
    nodes = [[], []]
    for h in range(4):
        merged = []
        for rhs in range(2):
            merged.append(
                jnp.concatenate(
                    [
                        picked[first + 8 * t : first + 8 * t + 8, rhs * 32 : rhs * 32 + 32]
                        for t in range(2**h)
                    ],
                    1,
                )
            )
        merged = jnp.concatenate(merged, 0)
        if h > 0:
            merged = dot3_ready(merged, stacks[h])
        nodes[0].append(merged[0:8])
        nodes[1].append(merged[8:16])
        first += 8 * 2**h
    local = []
    for rhs in range(2):
        across = jnp.concatenate(nodes[rhs], 0).T
        total = jnp.zeros((32, 32), F32)
        for a in range(32):
            total = total + blocks[32 * a : 32 * a + 32] * across[a : a + 1]
        total = total.T
        local.append(jnp.concatenate([jnp.sum(total[8 * h : 8 * h + 8], 0, keepdims=True) for h in range(4)], 1))
    return jnp.concatenate(local * 4, 0)


def descend(local, v_ref, w_ref, roots, four, merge):
    wide = dot3_ready(local, roots, NT)[0:2]
    for a in range(16):
        w_ref[pl.ds(a, 2, stride=16), 0:32] = wide[:, 32 * a : 32 * a + 32]
    wide = dot3_ready(w_ref[:, 0:32], four, NT)
    for rhs in range(2):
        for b in range(16):
            v_ref[pl.ds(2 * b + rhs, 16, stride=32), 0:32] = wide[
                16 * rhs : 16 * rhs + 16, 32 * b : 32 * b + 32
            ]
    return dot3_ready(v_ref[:, 0:32], merge, NT)


OFFSETS = [(a, b) for a in range(-3, 4) for b in range(-3, 4) if max(abs(a), abs(b)) >= 2]
BETAS = (-2, -1, 0, 1, 2, 3, 4, -3)
ROW_GROUPS = ((1, 2, 0, 3), (-3, -2, 5, 6, -1, 4))


def far_weights(coupling, blocks, window, w_hi, w_lo):
    for k in range(32):
        blocks[pl.ds(40 * k, 40), 0:32] = coupling[k].T
    window[...] = jnp.zeros_like(window)
    for number, (a, b) in enumerate(OFFSETS):
        block = blocks[pl.ds(number, 32, stride=40), :][:, 0:32]
        for at, beta in enumerate(BETAS):
            for side in range(2):
                if beta - 1 + side == b:
                    start = (a + 6) * 64 + side * 32
                    window[0, at, :, start : start + 32] = block
                    window[1, at, :, start + 64 : start + 96] = block
    row = 0
    for group in ROW_GROUPS:
        for shift in range(4):
            for i in group:
                for c in range(2):
                    start = (i + 3) * 64
                    odd = (start // 64) % 2
                    part = window[odd, 2 * shift + c, :, start + 64 * odd : start + 64 * odd + 256]
                    hi, lo = split(part)
                    w_hi[row : row + 32] = hi
                    w_lo[row : row + 32] = lo
                    row += 32


def far_field(coef, first, w_hi, w_lo, far):
    chunk = 128
    lanes = coef.shape[1]
    even = (iota((chunk, lanes), 1) & 32) == 0
    weights = pl.ds(first, 4 * lanes)
    for m in range(512 // chunk):
        at = 8 + m * chunk
        views = [coef[pl.ds(at + 2 * d, chunk)] for d in (-1, 0, 1)]
        views.append(jnp.where(even, coef[pl.ds(at + 4, chunk)], coef[pl.ds(at - 4, chunk)]))
        parts = [split(view) for view in views]
        hi = jnp.concatenate([part[0] for part in parts], 1)
        lo = jnp.concatenate([part[1] for part in parts], 1)
        total = dot(hi, w_hi[weights]) + dot(lo, w_hi[weights]) + dot(hi, w_lo[weights])
        rows = pl.ds(m * chunk, chunk)
        far[rows] = total if first == 0 else far[rows] + total


ORDER = ((3, 0, 1), (0, 1, 2))
CHUNK = 256


def shifted(taps, r):
    taps[r, 0, 528:544] = jnp.zeros((16, 256), BF16)
    taps[r, 1, 0:16] = jnp.zeros((16, 256), BF16)
    taps[r, 2, 16:528] = taps[r, 0, 18:530]
    taps[r, 3, 16:528] = taps[r, 1, 14:526]


def near_rows(taps, near, acc, i, rows, add):
    first, count = rows[0], len(rows)
    for c in range(2):
        for m in range(512 // CHUNK):
            span = pl.ds(16 + m * CHUNK, CHUNK)
            parts = [taps[i + a - 1, ORDER[c][b], span] for a in rows for b in range(3)]
            total = dot(jnp.concatenate(parts, 1), near[pl.ds(768 * first, 768 * count)])
            out = pl.ds(m * CHUNK, CHUNK)
            acc[i, c, out] = acc[i, c, out] + total if add else total


def kernel_main(
    n, x, near_any, coupling_any, top_any, valid, bt, transfer, partner_t, offset_t, count, acc, exps, mcol, hx, weight, near_out,
    xs, near, coupling, top_c, taps, edge_taps, basis, packed, inner_rows, outer, coef, coef_halo, hc, ho, table, blocks, window, w_hi, w_lo, far,
    v_ref, w_ref, path_ref, x_sem, w_sem, px_s, px_r, cf_s, cf_r, g_s, g_r
):
    me = lax.axis_index("region")
    right, left = lax.rem(me + 1, n), lax.rem(me + n - 1, n)
    group = me // 16
    spot = lax.rem(me, 16)
    core = lax.rem(me, 2)
    edge = 1 - core
    groups = n // 16
    barrier = pltpu.get_barrier_semaphore()
    peers1 = [group * 16 + lax.rem(spot + k, 16) for k in range(1, 16)]
    peers2 = [lax.rem(group + k, groups) * 16 + spot for k in range(1, groups)]

    def remote_copy(src, dst, send, recv, peer):
        return pltpu.make_async_remote_copy(
            src_ref=src, dst_ref=dst, send_sem=send, recv_sem=recv, device_id=(peer,), device_id_type=MESH
        )

    def remote(*args):
        copy = remote_copy(*args)
        copy.start()
        return copy

    for i in (0, 3, 1, 2):
        for c in range(2):
            for lt in range(2):
                local(x.at[i, :, c, :, pl.ds(lt * 128, 128)], xs.at[i, c, lt], x_sem.at[i])
    near_load = local(near_any, near, w_sem.at[0])
    coupling_load = local(coupling_any, coupling, w_sem.at[1])
    top_load = local(top_any, top_c, w_sem.at[2])
    for peer in [left, right] + peers1 + peers2:
        pl.semaphore_signal(barrier, inc=1, device_id=(peer,), device_id_type=MESH)

    basis[...] = jnp.zeros_like(basis)
    for at, i in enumerate(IN_ORDER):
        for c in range(2):
            basis[pl.ds(at * 64 + c * 32, 32), pl.ds((i * 2 + c) * 256, 256)] = bt[...]
    paths = tree_paths(transfer)
    four = split(paths[3])
    merge_up = split(leaf_paths(paths[2], IN_ORDER, (0, 1)))
    rows = mask_rows(valid[...])
    for i in (0, 3, 1, 2):
        await_bytes(xs.at[i], x_sem.at[i])
        for c in range(2):
            col = column(rows[i : i + 1, c * 512 : c * 512 + 512]).astype(BF16)
            mcol[i, c] = col
            for lt in range(2):
                part = xs.at[i, c, lt].reshape(512, 128)[...]
                taps[i, c, 16:528, lt * 128 : lt * 128 + 128] = part * col
    pixels = jnp.concatenate([taps[i, c, 16:528] for i in range(4) for c in range(2)], 1)
    packed[...] = dot(pixels, basis[...], NT)
    top = climb(packed[...], v_ref, w_ref, merge_up, four)
    table[pl.ds(me, 1)] = jnp.concatenate([top[0:1], top[1:2], jnp.zeros((1, 64), F32)], 1).reshape(1, 1, 128)

    pl.semaphore_wait(barrier, 2 + 15 + groups - 1)
    mine = table.at[pl.ds(me, 1)]
    for peer in peers1:
        remote(mine, mine, g_s.at[0], g_r.at[0], peer)
    for k in range(2):
        row = packed[:, 128 + 64 * k : 192 + 64 * k]
        outer[k] = jnp.concatenate([row[0:256], row[256:512]], 1)
    inner_rows[...] = packed[:, 0:128]
    coef_copies = [
        remote(inner_rows, hc.at[0], cf_s.at[0], cf_r.at[0], right),
        remote(inner_rows, hc.at[1], cf_s.at[1], cf_r.at[1], left),
        remote(outer.at[1], ho.at[0], cf_s.at[2], cf_r.at[2], right),
        remote(outer.at[0], ho.at[1], cf_s.at[3], cf_r.at[3], left),
    ]
    inside = pl.ds(16, 512)
    to_right = remote_copy(taps.at[3, pl.ds(0, 2), inside], hx.at[0], px_s.at[0], px_r.at[0], right)
    to_left = remote_copy(taps.at[0, pl.ds(0, 2), inside], hx.at[1], px_s.at[1], px_r.at[1], left)

    @pl.when(core == 0)
    def _():
        to_right.start()

    @pl.when(core == 1)
    def _():
        to_left.start()

    weight[...] = jnp.zeros_like(weight)
    for i2 in range(2):
        for c in range(2):
            start = (1 - i2) * 64 + (1 - c) * 32
            weight[i2, c, pl.ds(start, 32)] = bt[...]
            weight[i2, c, pl.ds(128 + start, 32)] = bt[...]
    for r in range(4):
        shifted(taps, r)
    near_load.wait()
    near_out[...] = near[pl.ds(pl.multiple_of(1536 * core, 256), 768)]
    near_rows(taps, near, acc, 1, (0, 1, 2), False)
    near_rows(taps, near, acc, 2, (0, 1, 2), False)
    near_rows(taps, near, acc, 0, (1, 2), False)
    near_rows(taps, near, acc, 3, (0, 1), False)
    coupling_load.wait()
    far_weights(coupling, blocks, window, w_hi, w_lo)
    coef[0:8] = jnp.zeros((8, 256), F32)
    coef[520:528] = jnp.zeros((8, 256), F32)
    coef[8:520] = packed[...]
    far_field(coef, 0, w_hi, w_lo, far)

    await_bytes(table.at[pl.ds(0, 15)], g_r.at[0])
    block = table.at[pl.ds(group * 16, 16)]
    for peer in peers2:
        remote(block, block, g_s.at[1], g_r.at[1], peer)

    @pl.when(core == 1)
    def _():
        to_right.start()

    @pl.when(core == 0)
    def _():
        to_left.start()

    top_load.wait()
    slots = top_blocks(me, offset_t, top_c)
    pick = top_picks(me, partner_t, count)
    stacks = (None,) + tuple(split(path) for path in paths[:3])
    roots = split(root_paths(me, paths, path_ref))
    merge_down = split(leaf_paths(paths[2], (3, 2, 1, 0), (1, 0)))

    await_bytes(hx.at[0], px_r.at[edge])
    edge_taps[0, 0, inside] = hx[edge, 0]
    edge_taps[0, 1, inside] = hx[edge, 1]
    shifted(edge_taps, 0)
    for c in range(2):
        for m in range(512 // CHUNK):
            parts = [edge_taps[0, ORDER[c][b], pl.ds(16 + m * CHUNK, CHUNK)] for b in range(3)]
            rows = pl.ds(m * CHUNK, CHUNK)
            begin = pl.multiple_of(1536 * edge, 256)
            acc[3 * edge, c, rows] += dot(jnp.concatenate(parts, 1), near[pl.ds(begin, 768)])

    for copy in coef_copies:
        copy.wait()
    coef_halo[0:8] = jnp.zeros((8, 384), F32)
    coef_halo[520:528] = jnp.zeros((8, 384), F32)
    for k, inner in enumerate((jnp.where(me > 0, 1.0, 0.0), jnp.where(me < n - 1, 1.0, 0.0))):
        coef_halo[8:520, 128 * k : 128 * k + 128] = hc[k] * inner
        start = 256 + 64 * k
        row = ho[k] * inner
        coef_halo[8:264, start : start + 64] = row[:, 0:64]
        coef_halo[264:520, start : start + 64] = row[:, 64:128]
    far_field(coef_halo, 1024, w_hi, w_lo, far)

    await_bytes(table.at[pl.ds(0, n - 16)], g_r.at[1])
    local_exp = top_expand(table.reshape(n, 128)[...], pick, slots, stacks)
    leaf = descend(local_exp, v_ref, w_ref, roots, four, merge_down) + far[...]
    hi, lo = split(leaf)
    for half in range(2):
        exps[half, :, 0:128] = hi[:, half * 128 : half * 128 + 128]
        exps[half, :, 128:256] = lo[:, half * 128 : half * 128 + 128]
    await_bytes(hx.at[0], px_r.at[core])
    await_bytes(hx.at[0], px_s.at[0])
    await_bytes(hx.at[0], px_s.at[1])
    await_bytes(table.at[pl.ds(0, 15)], g_s.at[0])
    await_bytes(table.at[pl.ds(0, n - 16)], g_s.at[1])


def kernel_out(n, acc, exps, mcol, hx, weight, near, out, taps, os, out_sem):
    me = lax.axis_index("region")
    edge = lax.rem(me, 2)
    for at, (i, side) in enumerate(((1, 1), (2, 0), (3 - 3 * edge, 1 - edge), (3 * edge, edge))):
        half = 1 - side if at >= 2 else 1 - i // 2
        if at == 3:
            inner = jnp.where(edge == 0, me > 0, me < n - 1).astype(F32).astype(BF16)
            for c in range(2):
                taps[0, c, 16:528] = hx[edge, c] * inner
            shifted(taps, 0)
        for c in range(2):
            total = acc[i, c] + dot(exps[half], weight[side, c])
            if at == 3:
                parts = [taps[0, ORDER[c][b], 16:528] for b in range(3)]
                total = total + dot(jnp.concatenate(parts, 1), near[...])
            col = mcol[i, c].astype(F32)
            for lt in range(2):
                os.at[at, c, lt].reshape(512, 128)[...] = total[:, lt * 128 : lt * 128 + 128] * col
                local(os.at[at, c, lt], out.at[i, :, c, :, pl.ds(lt * 128, 128)], out_sem.at[0])
    await_bytes(os, out_sem.at[0])


def body(n, pixels, valid, basis, near, transfer, coupling, top_c, partner, offset, count):
    x = pixels.reshape(4, 256, 2, 2, 256)
    bt = basis.T
    near = near.reshape(2304, 256)
    vmem = pl.BlockSpec(memory_space=pltpu.VMEM)
    anywhere = pl.BlockSpec(memory_space=pl.ANY)
    sds = jax.ShapeDtypeStruct
    dma = pltpu.SemaphoreType.DMA
    passed = pl.pallas_call(
        functools.partial(kernel_main, n),
        out_shape=(
            pltpu.VMEM((4, 2, 512, 256), F32), pltpu.VMEM((2, 512, 256), BF16), pltpu.VMEM((4, 2, 512, 128), BF16),
            pltpu.VMEM((2, 2, 512, 256), BF16),
            pltpu.VMEM((2, 2, 256, 256), BF16),
            pltpu.VMEM((768, 256), BF16),
        ),
        in_specs=[anywhere] * 4 + [vmem] * 5 + [pl.BlockSpec(memory_space=pltpu.SMEM)],
        out_specs=(vmem,) * 6,
        scratch_shapes=[
            pltpu.VMEM((4, 2, 2, 256, 2, 128), BF16),
            pltpu.VMEM((2304, 256), BF16),
            pltpu.VMEM((32, 32, 40), F32),
            pltpu.VMEM((32, 32, 160), F32),
            pltpu.VMEM((4, 4, 544, 256), BF16),
            pltpu.VMEM((1, 4, 544, 256), BF16),
            pltpu.VMEM((256, 2048), BF16),
            pltpu.VMEM((512, 256), F32),
            pltpu.VMEM((512, 128), F32),
            pltpu.VMEM((2, 256, 128), F32),
            pltpu.VMEM((528, 256), F32),
            pltpu.VMEM((528, 384), F32),
            pltpu.VMEM((2, 512, 128), F32),
            pltpu.VMEM((2, 256, 128), F32),
            pltpu.VMEM((n, 1, 128), F32),
            pltpu.VMEM((1280, 128), F32),
            pltpu.VMEM((2, 8, 32, 1024), F32),
            pltpu.VMEM((2560, 256), BF16),
            pltpu.VMEM((2560, 256), BF16),
            pltpu.VMEM((512, 256), F32),
            pltpu.VMEM((512, 128), F32),
            pltpu.VMEM((32, 128), F32),
            pltpu.VMEM((448, 128), F32),
            dma((4,)),
            dma((3,)),
            dma((4,)),
            dma((4,)),
            dma((4,)),
            dma((4,)),
            dma((2,)),
            dma((2,)),
        ],
        compiler_params=pltpu.CompilerParams(collective_id=0, has_side_effects=True, vmem_limit_bytes=VMEM_LIMIT),
    )(
        x, near, jnp.transpose(coupling, (1, 2, 0)), jnp.transpose(top_c, (1, 2, 0)),
        valid, bt, transfer, partner.T, offset.T, count,
    )
    out = pl.pallas_call(
        functools.partial(kernel_out, n),
        out_shape=sds((4, 256, 2, 2, 256), F32),
        in_specs=[vmem] * 6,
        out_specs=anywhere,
        scratch_shapes=[
            pltpu.VMEM((1, 4, 544, 256), BF16),
            pltpu.VMEM((4, 2, 2, 256, 2, 128), F32),
            dma((1,)),
        ],
        compiler_params=pltpu.CompilerParams(vmem_limit_bytes=24 << 20),
    )(*(pltpu.with_memory_space_constraint(a, pltpu.VMEM) for a in passed))
    return out.reshape(4, 512, 2, 256)


def solution(mesh):
    n = mesh.shape["region"]
    in_specs = (P("region", None, None, None), P("region", None)) + (P(),) * 8
    out_specs = P("region", None, None, None)
    return jax.shard_map(functools.partial(body, n), mesh=mesh, in_specs=in_specs, out_specs=out_specs, check_vma=False)
```

```python
import functools

import jax
import jax.numpy as jnp
from jax import lax
from jax.experimental import pallas as pl
from jax.experimental.pallas import tpu as pltpu
from jax.sharding import PartitionSpec as P

MESH = pl.DeviceIdType.MESH
F32 = jnp.float32
BF16 = jnp.bfloat16
NN = (((1,), (0,)), ((), ()))
NT = (((1,), (1,)), ((), ()))
IN_ORDER = (1, 2, 0, 3)
VMEM_LIMIT = 56 << 20


def dot(a, b, dims=NN):
    return lax.dot_general(a, b, dims, preferred_element_type=F32)


def split(x):
    hi = x.astype(BF16)
    return hi, (x - hi.astype(F32)).astype(BF16)


def dot3(a, b, dims=NN):
    a_hi, a_lo = split(a)
    b_hi, b_lo = split(b)
    return dot(a_hi, b_hi, dims) + (dot(a_lo, b_hi, dims) + dot(a_hi, b_lo, dims))


def dot3_ready(a, b, dims=NN):
    a_hi, a_lo = split(a)
    return dot(a_hi, b[0], dims) + (dot(a_lo, b[0], dims) + dot(a_hi, b[1], dims))


def iota(shape, axis):
    return lax.broadcasted_iota(jnp.int32, shape, axis)


def local(src, dst, sem):
    copy = pltpu.make_async_copy(src, dst, sem)
    copy.start()
    return copy


def await_bytes(ref, sem):
    pltpu.make_async_copy(ref, ref, sem).wait()


def tree_paths(transfer):
    side0, side1 = transfer[0], transfer[1]
    both = jnp.concatenate([side0, side1], 0)
    lanes = jnp.concatenate([side0, side1], 1)
    pairs = dot3(both, lanes)
    two = jnp.concatenate([pairs[:, :32], pairs[:, 32:]], 0)
    three = dot3(two, lanes)
    three = jnp.concatenate([three[:, :32], three[:, 32:]], 0)
    two_lanes = jnp.concatenate([two[32 * s : 32 * s + 32] for s in range(4)], 1)
    four = dot3(two, two_lanes)
    four = jnp.concatenate([four[:, 32 * s : 32 * s + 32] for s in range(4)], 0)
    return both, two, three, four


def mask_rows(valid):
    values = valid.astype(F32).astype(BF16)
    values = jnp.concatenate([values, values], 0)
    lane = iota((512, 1024), 1)
    leaf = (lane & 510) + (lane >> 9)
    pick = (iota((512, 1024), 0) == leaf).astype(F32).astype(BF16)
    return dot(values, pick)


def column(row):
    return jnp.concatenate(
        [jnp.broadcast_to(row[:, 128 * b : 128 * b + 128], (128, 128)).T for b in range(4)], 0
    )


def leaf_paths(three, rows, sides):
    return jnp.concatenate(
        [three[(c * 4 + i) * 32 : (c * 4 + i) * 32 + 32] for i in rows for c in sides], 0
    )


def climb(packed, v_ref, w_ref, merge, four):
    v_ref[:, 0:32] = dot3_ready(packed, merge)
    rows = []
    for rhs in range(2):
        rows.append(
            jnp.concatenate(
                [v_ref[pl.ds(2 * b + rhs, 16, stride=32), :][:, 0:32] for b in range(16)], 1
            )
        )
    w_ref[:, 0:32] = dot3_ready(jnp.concatenate(rows, 0), four)
    last = jnp.concatenate([w_ref[pl.ds(a, 2, stride=16), :][:, 0:32] for a in range(16)], 1)
    return dot3_ready(jnp.concatenate([last, last, last, last], 0), four)[0:2]


def top_blocks(me, offset_t, top_c):
    bases = (0, 256, 384, 448)
    lane = iota((8, 480), 1)
    offsets = offset_t[...].astype(F32)
    picks = []
    for h in range(4):
        chosen = jnp.sum(jnp.where(lane == bases[h] + (me >> h), offsets, 0.0), 1, keepdims=True)
        picks.append((iota((8, 160), 1).astype(F32) == chosen).astype(F32))
    pick = jnp.concatenate(picks, 0).astype(BF16)
    hi, lo = split(top_c[...].reshape(1024, 160))
    return dot(hi, pick, NT) + dot(lo, pick, NT)


def top_picks(me, partner_t, count):
    bases = (0, 256, 384, 448)
    lane = iota((8, 480), 1)
    slot = iota((8, 256), 0)
    partners = partner_t[...].astype(F32)
    node = iota((8, 256), 1).astype(F32)
    picks = []
    for h in range(4):
        row = bases[h] + (me >> h)
        chosen = jnp.sum(jnp.where(lane == row, partners, 0.0), 1, keepdims=True) - bases[h]
        live = slot < count[row]
        for t in range(2**h):
            picks.append(jnp.where(live & (node == chosen * 2**h + t), 1.0, 0.0))
    return jnp.concatenate(picks, 0).astype(BF16)


def root_paths(me, paths, path_ref):
    both, two, three, four = paths
    path_ref[0:64, 0:32] = both
    path_ref[64:192, 0:32] = two
    path_ref[192:448, 0:32] = three
    starts = (0, 0, 64, 192)
    parts = [four]
    for h in range(1, 4):
        begin = pl.multiple_of(starts[h] + (me & (2**h - 1)) * 32, 32)
        parts.append(dot3(four, path_ref[pl.ds(begin, 32), :][:, 0:32]))
    return jnp.concatenate(parts, 1)


def top_expand(table, pick, blocks, stacks):
    hi, lo = split(table)
    picked = dot(pick, hi) + dot(pick, lo)
    first = 0
    nodes = [[], []]
    for h in range(4):
        merged = []
        for rhs in range(2):
            merged.append(
                jnp.concatenate(
                    [
                        picked[first + 8 * t : first + 8 * t + 8, rhs * 32 : rhs * 32 + 32]
                        for t in range(2**h)
                    ],
                    1,
                )
            )
        merged = jnp.concatenate(merged, 0)
        if h > 0:
            merged = dot3_ready(merged, stacks[h])
        nodes[0].append(merged[0:8])
        nodes[1].append(merged[8:16])
        first += 8 * 2**h
    local = []
    for rhs in range(2):
        across = jnp.concatenate(nodes[rhs], 0).T
        total = jnp.zeros((32, 32), F32)
        for a in range(32):
            total = total + blocks[32 * a : 32 * a + 32] * across[a : a + 1]
        total = total.T
        local.append(jnp.concatenate([jnp.sum(total[8 * h : 8 * h + 8], 0, keepdims=True) for h in range(4)], 1))
    return jnp.concatenate(local * 4, 0)


def descend(local, v_ref, w_ref, roots, four, merge):
    wide = dot3_ready(local, roots, NT)[0:2]
    for a in range(16):
        w_ref[pl.ds(a, 2, stride=16), 0:32] = wide[:, 32 * a : 32 * a + 32]
    wide = dot3_ready(w_ref[:, 0:32], four, NT)
    for rhs in range(2):
        for b in range(16):
            v_ref[pl.ds(2 * b + rhs, 16, stride=32), 0:32] = wide[
                16 * rhs : 16 * rhs + 16, 32 * b : 32 * b + 32
            ]
    return dot3_ready(v_ref[:, 0:32], merge, NT)


OFFSETS = [(a, b) for a in range(-3, 4) for b in range(-3, 4) if max(abs(a), abs(b)) >= 2]
BETAS = (-2, -1, 0, 1, 2, 3, 4, -3)
ROW_GROUPS = ((1, 2, 0, 3), (-3, -2, 5, 6, -1, 4))


def far_weights(coupling, blocks, window, w_hi, w_lo):
    for k in range(32):
        blocks[pl.ds(40 * k, 40), 0:32] = coupling[k].T
    window[...] = jnp.zeros_like(window)
    for number, (a, b) in enumerate(OFFSETS):
        block = blocks[pl.ds(number, 32, stride=40), :][:, 0:32]
        for at, beta in enumerate(BETAS):
            for side in range(2):
                if beta - 1 + side == b:
                    start = (a + 6) * 64 + side * 32
                    window[0, at, :, start : start + 32] = block
                    window[1, at, :, start + 64 : start + 96] = block
    row = 0
    for group in ROW_GROUPS:
        for shift in range(4):
            for i in group:
                for c in range(2):
                    start = (i + 3) * 64
                    odd = (start // 64) % 2
                    part = window[odd, 2 * shift + c, :, start + 64 * odd : start + 64 * odd + 256]
                    hi, lo = split(part)
                    w_hi[row : row + 32] = hi
                    w_lo[row : row + 32] = lo
                    row += 32


def far_field(coef, first, w_hi, w_lo, far):
    chunk = 128
    lanes = coef.shape[1]
    even = (iota((chunk, lanes), 1) & 32) == 0
    weights = pl.ds(first, 4 * lanes)
    for m in range(512 // chunk):
        at = 8 + m * chunk
        views = [coef[pl.ds(at + 2 * d, chunk)] for d in (-1, 0, 1)]
        views.append(jnp.where(even, coef[pl.ds(at + 4, chunk)], coef[pl.ds(at - 4, chunk)]))
        parts = [split(view) for view in views]
        hi = jnp.concatenate([part[0] for part in parts], 1)
        lo = jnp.concatenate([part[1] for part in parts], 1)
        total = dot(hi, w_hi[weights]) + dot(lo, w_hi[weights]) + dot(hi, w_lo[weights])
        rows = pl.ds(m * chunk, chunk)
        far[rows] = total if first == 0 else far[rows] + total


ORDER = ((3, 0, 1), (0, 1, 2))
CHUNK = 256


def shifted(taps, r):
    taps[r, 0, 528:544] = jnp.zeros((16, 256), BF16)
    taps[r, 1, 0:16] = jnp.zeros((16, 256), BF16)
    taps[r, 2, 16:528] = taps[r, 0, 18:530]
    taps[r, 3, 16:528] = taps[r, 1, 14:526]


def near_rows(taps, near, acc, i, rows, add):
    first, count = rows[0], len(rows)
    for c in range(2):
        for m in range(512 // CHUNK):
            span = pl.ds(16 + m * CHUNK, CHUNK)
            parts = [taps[i + a - 1, ORDER[c][b], span] for a in rows for b in range(3)]
            total = dot(jnp.concatenate(parts, 1), near[pl.ds(768 * first, 768 * count)])
            out = pl.ds(m * CHUNK, CHUNK)
            acc[i, c, out] = acc[i, c, out] + total if add else total


def kernel_main(
    n, x, near_any, coupling_any, top_any, valid, bt, transfer, partner_t, offset_t, count, acc, exps, mcol, hx, weight, near_out,
    xs, near, coupling, top_c, taps, edge_taps, basis, packed, inner_rows, outer, coef, coef_halo, hc, ho, table, blocks, window, w_hi, w_lo, far,
    v_ref, w_ref, path_ref, x_sem, w_sem, px_s, px_r, cf_s, cf_r, g_s, g_r
):
    me = lax.axis_index("region")
    right, left = lax.rem(me + 1, n), lax.rem(me + n - 1, n)
    group = me // 16
    spot = lax.rem(me, 16)
    core = lax.rem(me, 2)
    edge = 1 - core
    groups = n // 16
    barrier = pltpu.get_barrier_semaphore()
    peers1 = [group * 16 + lax.rem(spot + k, 16) for k in range(1, 16)]
    peers2 = [lax.rem(group + k, groups) * 16 + spot for k in range(1, groups)]

    def remote_copy(src, dst, send, recv, peer):
        return pltpu.make_async_remote_copy(
            src_ref=src, dst_ref=dst, send_sem=send, recv_sem=recv, device_id=(peer,), device_id_type=MESH
        )

    def remote(*args):
        copy = remote_copy(*args)
        copy.start()
        return copy

    for i in (0, 3, 1, 2):
        for c in range(2):
            for lt in range(2):
                local(x.at[i, :, c, :, pl.ds(lt * 128, 128)], xs.at[i, c, lt], x_sem.at[i])
    near_load = local(near_any, near, w_sem.at[0])
    coupling_load = local(coupling_any, coupling, w_sem.at[1])
    top_load = local(top_any, top_c, w_sem.at[2])
    for peer in [left, right] + peers1 + peers2:
        pl.semaphore_signal(barrier, inc=1, device_id=(peer,), device_id_type=MESH)

    basis[...] = jnp.zeros_like(basis)
    for at, i in enumerate(IN_ORDER):
        for c in range(2):
            basis[pl.ds(at * 64 + c * 32, 32), pl.ds((i * 2 + c) * 256, 256)] = bt[...]
    paths = tree_paths(transfer)
    four = split(paths[3])
    merge_up = split(leaf_paths(paths[2], IN_ORDER, (0, 1)))
    rows = mask_rows(valid[...])
    for i in (0, 3, 1, 2):
        await_bytes(xs.at[i], x_sem.at[i])
        for c in range(2):
            col = column(rows[i : i + 1, c * 512 : c * 512 + 512]).astype(BF16)
            mcol[i, c] = col
            for lt in range(2):
                part = xs.at[i, c, lt].reshape(512, 128)[...]
                taps[i, c, 16:528, lt * 128 : lt * 128 + 128] = part * col
    pixels = jnp.concatenate([taps[i, c, 16:528] for i in range(4) for c in range(2)], 1)
    packed[...] = dot(pixels, basis[...], NT)
    top = climb(packed[...], v_ref, w_ref, merge_up, four)
    table[pl.ds(me, 1)] = jnp.concatenate([top[0:1], top[1:2], jnp.zeros((1, 64), F32)], 1).reshape(1, 1, 128)

    pl.semaphore_wait(barrier, 2 + 15 + groups - 1)
    mine = table.at[pl.ds(me, 1)]
    for peer in peers1:
        remote(mine, mine, g_s.at[0], g_r.at[0], peer)
    for k in range(2):
        row = packed[:, 128 + 64 * k : 192 + 64 * k]
        outer[k] = jnp.concatenate([row[0:256], row[256:512]], 1)
    inner_rows[...] = packed[:, 0:128]
    coef_copies = [
        remote(inner_rows, hc.at[0], cf_s.at[0], cf_r.at[0], right),
        remote(inner_rows, hc.at[1], cf_s.at[1], cf_r.at[1], left),
        remote(outer.at[1], ho.at[0], cf_s.at[2], cf_r.at[2], right),
        remote(outer.at[0], ho.at[1], cf_s.at[3], cf_r.at[3], left),
    ]
    inside = pl.ds(16, 512)
    to_right = remote_copy(taps.at[3, pl.ds(0, 2), inside], hx.at[0], px_s.at[0], px_r.at[0], right)
    to_left = remote_copy(taps.at[0, pl.ds(0, 2), inside], hx.at[1], px_s.at[1], px_r.at[1], left)

    @pl.when(core == 0)
    def _():
        to_right.start()

    @pl.when(core == 1)
    def _():
        to_left.start()

    weight[...] = jnp.zeros_like(weight)
    for i2 in range(2):
        for c in range(2):
            start = (1 - i2) * 64 + (1 - c) * 32
            weight[i2, c, pl.ds(start, 32)] = bt[...]
            weight[i2, c, pl.ds(128 + start, 32)] = bt[...]
    for r in range(4):
        shifted(taps, r)
    near_load.wait()
    near_out[...] = near[pl.ds(pl.multiple_of(1536 * core, 256), 768)]
    near_rows(taps, near, acc, 1, (0, 1, 2), False)
    near_rows(taps, near, acc, 2, (0, 1, 2), False)
    near_rows(taps, near, acc, 0, (1, 2), False)
    near_rows(taps, near, acc, 3, (0, 1), False)
    coupling_load.wait()
    far_weights(coupling, blocks, window, w_hi, w_lo)

    await_bytes(table.at[pl.ds(0, 15)], g_r.at[0])
    block = table.at[pl.ds(group * 16, 16)]
    for peer in peers2:
        remote(block, block, g_s.at[1], g_r.at[1], peer)

    @pl.when(core == 1)
    def _():
        to_right.start()

    @pl.when(core == 0)
    def _():
        to_left.start()

    coef[0:8] = jnp.zeros((8, 256), F32)
    coef[520:528] = jnp.zeros((8, 256), F32)
    coef[8:520] = packed[...]
    far_field(coef, 0, w_hi, w_lo, far)
    top_load.wait()
    slots = top_blocks(me, offset_t, top_c)
    pick = top_picks(me, partner_t, count)
    stacks = (None,) + tuple(split(path) for path in paths[:3])
    roots = split(root_paths(me, paths, path_ref))
    merge_down = split(leaf_paths(paths[2], (3, 2, 1, 0), (1, 0)))

    await_bytes(hx.at[0], px_r.at[edge])
    edge_taps[0, 0, inside] = hx[edge, 0]
    edge_taps[0, 1, inside] = hx[edge, 1]
    shifted(edge_taps, 0)
    for c in range(2):
        for m in range(512 // CHUNK):
            parts = [edge_taps[0, ORDER[c][b], pl.ds(16 + m * CHUNK, CHUNK)] for b in range(3)]
            rows = pl.ds(m * CHUNK, CHUNK)
            begin = pl.multiple_of(1536 * edge, 256)
            acc[3 * edge, c, rows] += dot(jnp.concatenate(parts, 1), near[pl.ds(begin, 768)])

    for copy in coef_copies:
        copy.wait()
    coef_halo[0:8] = jnp.zeros((8, 384), F32)
    coef_halo[520:528] = jnp.zeros((8, 384), F32)
    for k, inner in enumerate((jnp.where(me > 0, 1.0, 0.0), jnp.where(me < n - 1, 1.0, 0.0))):
        coef_halo[8:520, 128 * k : 128 * k + 128] = hc[k] * inner
        start = 256 + 64 * k
        row = ho[k] * inner
        coef_halo[8:264, start : start + 64] = row[:, 0:64]
        coef_halo[264:520, start : start + 64] = row[:, 64:128]
    far_field(coef_halo, 1024, w_hi, w_lo, far)

    await_bytes(table.at[pl.ds(0, n - 16)], g_r.at[1])
    local_exp = top_expand(table.reshape(n, 128)[...], pick, slots, stacks)
    leaf = descend(local_exp, v_ref, w_ref, roots, four, merge_down) + far[...]
    hi, lo = split(leaf)
    for half in range(2):
        exps[half, :, 0:128] = hi[:, half * 128 : half * 128 + 128]
        exps[half, :, 128:256] = lo[:, half * 128 : half * 128 + 128]
    await_bytes(hx.at[0], px_r.at[core])
    await_bytes(hx.at[0], px_s.at[0])
    await_bytes(hx.at[0], px_s.at[1])
    await_bytes(table.at[pl.ds(0, 15)], g_s.at[0])
    await_bytes(table.at[pl.ds(0, n - 16)], g_s.at[1])


def kernel_out(n, acc, exps, mcol, hx, weight, near, out, taps, os, out_sem):
    me = lax.axis_index("region")
    edge = lax.rem(me, 2)
    for at, (i, side) in enumerate(((1, 1), (2, 0), (3 - 3 * edge, 1 - edge), (3 * edge, edge))):
        half = 1 - side if at >= 2 else 1 - i // 2
        if at == 3:
            inner = jnp.where(edge == 0, me > 0, me < n - 1).astype(F32).astype(BF16)
            for c in range(2):
                taps[0, c, 16:528] = hx[edge, c] * inner
            shifted(taps, 0)
        for c in range(2):
            total = acc[i, c] + dot(exps[half], weight[side, c])
            if at == 3:
                parts = [taps[0, ORDER[c][b], 16:528] for b in range(3)]
                total = total + dot(jnp.concatenate(parts, 1), near[...])
            col = mcol[i, c].astype(F32)
            for lt in range(2):
                os.at[at, c, lt].reshape(512, 128)[...] = total[:, lt * 128 : lt * 128 + 128] * col
                local(os.at[at, c, lt], out.at[i, :, c, :, pl.ds(lt * 128, 128)], out_sem.at[0])
    await_bytes(os, out_sem.at[0])


def body(n, pixels, valid, basis, near, transfer, coupling, top_c, partner, offset, count):
    x = pixels.reshape(4, 256, 2, 2, 256)
    bt = basis.T
    near = near.reshape(2304, 256)
    vmem = pl.BlockSpec(memory_space=pltpu.VMEM)
    anywhere = pl.BlockSpec(memory_space=pl.ANY)
    sds = jax.ShapeDtypeStruct
    dma = pltpu.SemaphoreType.DMA
    passed = pl.pallas_call(
        functools.partial(kernel_main, n),
        out_shape=(
            pltpu.VMEM((4, 2, 512, 256), F32), pltpu.VMEM((2, 512, 256), BF16), pltpu.VMEM((4, 2, 512, 128), BF16),
            pltpu.VMEM((2, 2, 512, 256), BF16),
            pltpu.VMEM((2, 2, 256, 256), BF16),
            pltpu.VMEM((768, 256), BF16),
        ),
        in_specs=[anywhere] * 4 + [vmem] * 5 + [pl.BlockSpec(memory_space=pltpu.SMEM)],
        out_specs=(vmem,) * 6,
        scratch_shapes=[
            pltpu.VMEM((4, 2, 2, 256, 2, 128), BF16),
            pltpu.VMEM((2304, 256), BF16),
            pltpu.VMEM((32, 32, 40), F32),
            pltpu.VMEM((32, 32, 160), F32),
            pltpu.VMEM((4, 4, 544, 256), BF16),
            pltpu.VMEM((1, 4, 544, 256), BF16),
            pltpu.VMEM((256, 2048), BF16),
            pltpu.VMEM((512, 256), F32),
            pltpu.VMEM((512, 128), F32),
            pltpu.VMEM((2, 256, 128), F32),
            pltpu.VMEM((528, 256), F32),
            pltpu.VMEM((528, 384), F32),
            pltpu.VMEM((2, 512, 128), F32),
            pltpu.VMEM((2, 256, 128), F32),
            pltpu.VMEM((n, 1, 128), F32),
            pltpu.VMEM((1280, 128), F32),
            pltpu.VMEM((2, 8, 32, 1024), F32),
            pltpu.VMEM((2560, 256), BF16),
            pltpu.VMEM((2560, 256), BF16),
            pltpu.VMEM((512, 256), F32),
            pltpu.VMEM((512, 128), F32),
            pltpu.VMEM((32, 128), F32),
            pltpu.VMEM((448, 128), F32),
            dma((4,)),
            dma((3,)),
            dma((4,)),
            dma((4,)),
            dma((4,)),
            dma((4,)),
            dma((2,)),
            dma((2,)),
        ],
        compiler_params=pltpu.CompilerParams(collective_id=0, has_side_effects=True, vmem_limit_bytes=VMEM_LIMIT),
    )(
        x, near, jnp.transpose(coupling, (1, 2, 0)), jnp.transpose(top_c, (1, 2, 0)),
        valid, bt, transfer, partner.T, offset.T, count,
    )
    out = pl.pallas_call(
        functools.partial(kernel_out, n),
        out_shape=sds((4, 256, 2, 2, 256), F32),
        in_specs=[vmem] * 6,
        out_specs=anywhere,
        scratch_shapes=[
            pltpu.VMEM((1, 4, 544, 256), BF16),
            pltpu.VMEM((4, 2, 2, 256, 2, 128), F32),
            dma((1,)),
        ],
        compiler_params=pltpu.CompilerParams(vmem_limit_bytes=24 << 20),
    )(*(pltpu.with_memory_space_constraint(a, pltpu.VMEM) for a in passed))
    return out.reshape(4, 512, 2, 256)


def solution(mesh):
    n = mesh.shape["region"]
    in_specs = (P("region", None, None, None), P("region", None)) + (P(),) * 8
    out_specs = P("region", None, None, None)
    return jax.shard_map(functools.partial(body, n), mesh=mesh, in_specs=in_specs, out_specs=out_specs, check_vma=False)
```

```python
import functools

import jax
import jax.numpy as jnp
from jax import lax
from jax.experimental import pallas as pl
from jax.experimental.pallas import tpu as pltpu
from jax.sharding import PartitionSpec as P

MESH = pl.DeviceIdType.MESH
F32 = jnp.float32
BF16 = jnp.bfloat16
NN = (((1,), (0,)), ((), ()))
NT = (((1,), (1,)), ((), ()))
IN_ORDER = (1, 2, 0, 3)
VMEM_LIMIT = 56 << 20


def dot(a, b, dims=NN):
    return lax.dot_general(a, b, dims, preferred_element_type=F32)


def split(x):
    hi = x.astype(BF16)
    return hi, (x - hi.astype(F32)).astype(BF16)


def dot3(a, b, dims=NN):
    a_hi, a_lo = split(a)
    b_hi, b_lo = split(b)
    return dot(a_hi, b_hi, dims) + (dot(a_lo, b_hi, dims) + dot(a_hi, b_lo, dims))


def dot3_ready(a, b, dims=NN):
    a_hi, a_lo = split(a)
    return dot(a_hi, b[0], dims) + (dot(a_lo, b[0], dims) + dot(a_hi, b[1], dims))


def iota(shape, axis):
    return lax.broadcasted_iota(jnp.int32, shape, axis)


def local(src, dst, sem):
    copy = pltpu.make_async_copy(src, dst, sem)
    copy.start()
    return copy


def await_bytes(ref, sem):
    pltpu.make_async_copy(ref, ref, sem).wait()


def tree_paths(transfer):
    side0, side1 = transfer[0], transfer[1]
    both = jnp.concatenate([side0, side1], 0)
    lanes = jnp.concatenate([side0, side1], 1)
    pairs = dot3(both, lanes)
    two = jnp.concatenate([pairs[:, :32], pairs[:, 32:]], 0)
    three = dot3(two, lanes)
    three = jnp.concatenate([three[:, :32], three[:, 32:]], 0)
    two_lanes = jnp.concatenate([two[32 * s : 32 * s + 32] for s in range(4)], 1)
    four = dot3(two, two_lanes)
    four = jnp.concatenate([four[:, 32 * s : 32 * s + 32] for s in range(4)], 0)
    return both, two, three, four


def mask_rows(valid):
    values = valid.astype(F32).astype(BF16)
    values = jnp.concatenate([values, values], 0)
    lane = iota((512, 1024), 1)
    leaf = (lane & 510) + (lane >> 9)
    pick = (iota((512, 1024), 0) == leaf).astype(F32).astype(BF16)
    return dot(values, pick)


def column(row):
    return jnp.concatenate(
        [jnp.broadcast_to(row[:, 128 * b : 128 * b + 128], (128, 128)).T for b in range(4)], 0
    )


def leaf_paths(three, rows, sides):
    return jnp.concatenate(
        [three[(c * 4 + i) * 32 : (c * 4 + i) * 32 + 32] for i in rows for c in sides], 0
    )


def climb(packed, v_ref, w_ref, merge, four):
    v_ref[:, 0:32] = dot3_ready(packed, merge)
    rows = []
    for rhs in range(2):
        rows.append(
            jnp.concatenate(
                [v_ref[pl.ds(2 * b + rhs, 16, stride=32), :][:, 0:32] for b in range(16)], 1
            )
        )
    w_ref[:, 0:32] = dot3_ready(jnp.concatenate(rows, 0), four)
    last = jnp.concatenate([w_ref[pl.ds(a, 2, stride=16), :][:, 0:32] for a in range(16)], 1)
    return dot3_ready(jnp.concatenate([last, last, last, last], 0), four)[0:2]


def top_blocks(me, offset_t, top_c):
    bases = (0, 256, 384, 448)
    lane = iota((8, 480), 1)
    offsets = offset_t[...].astype(F32)
    picks = []
    for h in range(4):
        chosen = jnp.sum(jnp.where(lane == bases[h] + (me >> h), offsets, 0.0), 1, keepdims=True)
        picks.append((iota((8, 160), 1).astype(F32) == chosen).astype(F32))
    pick = jnp.concatenate(picks, 0).astype(BF16)
    hi, lo = split(top_c[...].reshape(1024, 160))
    return dot(hi, pick, NT) + dot(lo, pick, NT)


def top_picks(me, partner_t, count):
    bases = (0, 256, 384, 448)
    lane = iota((8, 480), 1)
    slot = iota((8, 256), 0)
    partners = partner_t[...].astype(F32)
    node = iota((8, 256), 1).astype(F32)
    picks = []
    for h in range(4):
        row = bases[h] + (me >> h)
        chosen = jnp.sum(jnp.where(lane == row, partners, 0.0), 1, keepdims=True) - bases[h]
        live = slot < count[row]
        for t in range(2**h):
            picks.append(jnp.where(live & (node == chosen * 2**h + t), 1.0, 0.0))
    return jnp.concatenate(picks, 0).astype(BF16)


def root_paths(me, paths, path_ref):
    both, two, three, four = paths
    path_ref[0:64, 0:32] = both
    path_ref[64:192, 0:32] = two
    path_ref[192:448, 0:32] = three
    starts = (0, 0, 64, 192)
    parts = [four]
    for h in range(1, 4):
        begin = pl.multiple_of(starts[h] + (me & (2**h - 1)) * 32, 32)
        parts.append(dot3(four, path_ref[pl.ds(begin, 32), :][:, 0:32]))
    return jnp.concatenate(parts, 1)


def top_expand(table, pick, blocks, stacks):
    hi, lo = split(table)
    picked = dot(pick, hi) + dot(pick, lo)
    first = 0
    nodes = [[], []]
    for h in range(4):
        merged = []
        for rhs in range(2):
            merged.append(
                jnp.concatenate(
                    [
                        picked[first + 8 * t : first + 8 * t + 8, rhs * 32 : rhs * 32 + 32]
                        for t in range(2**h)
                    ],
                    1,
                )
            )
        merged = jnp.concatenate(merged, 0)
        if h > 0:
            merged = dot3_ready(merged, stacks[h])
        nodes[0].append(merged[0:8])
        nodes[1].append(merged[8:16])
        first += 8 * 2**h
    local = []
    for rhs in range(2):
        across = jnp.concatenate(nodes[rhs], 0).T
        total = jnp.zeros((32, 32), F32)
        for a in range(32):
            total = total + blocks[32 * a : 32 * a + 32] * across[a : a + 1]
        total = total.T
        local.append(jnp.concatenate([jnp.sum(total[8 * h : 8 * h + 8], 0, keepdims=True) for h in range(4)], 1))
    return jnp.concatenate(local * 4, 0)


def descend(local, v_ref, w_ref, roots, four, merge):
    wide = dot3_ready(local, roots, NT)[0:2]
    for a in range(16):
        w_ref[pl.ds(a, 2, stride=16), 0:32] = wide[:, 32 * a : 32 * a + 32]
    wide = dot3_ready(w_ref[:, 0:32], four, NT)
    for rhs in range(2):
        for b in range(16):
            v_ref[pl.ds(2 * b + rhs, 16, stride=32), 0:32] = wide[
                16 * rhs : 16 * rhs + 16, 32 * b : 32 * b + 32
            ]
    return dot3_ready(v_ref[:, 0:32], merge, NT)


OFFSETS = [(a, b) for a in range(-3, 4) for b in range(-3, 4) if max(abs(a), abs(b)) >= 2]
BETAS = (-2, -1, 0, 1, 2, 3, 4, -3)
ROW_GROUPS = ((1, 2, 0, 3), (-3, -2, 5, 6, -1, 4))


def far_weights(coupling, blocks, window, w_hi, w_lo):
    for k in range(32):
        blocks[pl.ds(40 * k, 40), 0:32] = coupling[k].T
    window[...] = jnp.zeros_like(window)
    for number, (a, b) in enumerate(OFFSETS):
        block = blocks[pl.ds(number, 32, stride=40), :][:, 0:32]
        for at, beta in enumerate(BETAS):
            for side in range(2):
                if beta - 1 + side == b:
                    start = (a + 6) * 64 + side * 32
                    window[0, at, :, start : start + 32] = block
                    window[1, at, :, start + 64 : start + 96] = block
    row = 0
    for group in ROW_GROUPS:
        for shift in range(4):
            for i in group:
                for c in range(2):
                    start = (i + 3) * 64
                    odd = (start // 64) % 2
                    part = window[odd, 2 * shift + c, :, start + 64 * odd : start + 64 * odd + 256]
                    hi, lo = split(part)
                    w_hi[row : row + 32] = hi
                    w_lo[row : row + 32] = lo
                    row += 32


def far_field(coef, first, w_hi, w_lo, far):
    chunk = 128
    lanes = coef.shape[1]
    even = (iota((chunk, lanes), 1) & 32) == 0
    weights = pl.ds(first, 4 * lanes)
    for m in range(512 // chunk):
        at = 8 + m * chunk
        views = [coef[pl.ds(at + 2 * d, chunk)] for d in (-1, 0, 1)]
        views.append(jnp.where(even, coef[pl.ds(at + 4, chunk)], coef[pl.ds(at - 4, chunk)]))
        parts = [split(view) for view in views]
        hi = jnp.concatenate([part[0] for part in parts], 1)
        lo = jnp.concatenate([part[1] for part in parts], 1)
        total = dot(hi, w_hi[weights]) + dot(lo, w_hi[weights]) + dot(hi, w_lo[weights])
        rows = pl.ds(m * chunk, chunk)
        far[rows] = total if first == 0 else far[rows] + total


ORDER = ((3, 0, 1), (0, 1, 2))
CHUNK = 256


def shifted(taps, r):
    taps[r, 0, 528:544] = jnp.zeros((16, 256), BF16)
    taps[r, 1, 0:16] = jnp.zeros((16, 256), BF16)
    taps[r, 2, 16:528] = taps[r, 0, 18:530]
    taps[r, 3, 16:528] = taps[r, 1, 14:526]


def near_rows(taps, near, acc, i, rows, add):
    first, count = rows[0], len(rows)
    for c in range(2):
        for m in range(512 // CHUNK):
            span = pl.ds(16 + m * CHUNK, CHUNK)
            parts = [taps[i + a - 1, ORDER[c][b], span] for a in rows for b in range(3)]
            total = dot(jnp.concatenate(parts, 1), near[pl.ds(768 * first, 768 * count)])
            out = pl.ds(m * CHUNK, CHUNK)
            acc[i, c, out] = acc[i, c, out] + total if add else total


def kernel_main(
    n, x, near_any, coupling_any, top_any, valid, bt, transfer, partner_t, offset_t, count, acc, exps, mcol, hx, weight, near_out,
    xs, near, coupling, top_c, taps, edge_taps, basis, packed, inner_rows, outer, coef, coef_halo, hc, ho, table, blocks, window, w_hi, w_lo, far,
    v_ref, w_ref, path_ref, x_sem, w_sem, px_s, px_r, cf_s, cf_r, g_s, g_r
):
    me = lax.axis_index("region")
    right, left = lax.rem(me + 1, n), lax.rem(me + n - 1, n)
    group = me // 16
    spot = lax.rem(me, 16)
    core = lax.rem(me, 2)
    edge = 1 - core
    groups = n // 16
    barrier = pltpu.get_barrier_semaphore()
    peers1 = [group * 16 + lax.rem(spot + k, 16) for k in range(1, 16)]
    peers2 = [lax.rem(group + k, groups) * 16 + spot for k in range(1, groups)]

    def remote_copy(src, dst, send, recv, peer):
        return pltpu.make_async_remote_copy(
            src_ref=src, dst_ref=dst, send_sem=send, recv_sem=recv, device_id=(peer,), device_id_type=MESH
        )

    def remote(*args):
        copy = remote_copy(*args)
        copy.start()
        return copy

    for i in (0, 3, 1, 2):
        for c in range(2):
            for lt in range(2):
                local(x.at[i, :, c, :, pl.ds(lt * 128, 128)], xs.at[i, c, lt], x_sem.at[i])
    for peer in [left, right] + peers1 + peers2:
        pl.semaphore_signal(barrier, inc=1, device_id=(peer,), device_id_type=MESH)
    near_load = local(near_any, near, w_sem.at[0])
    coupling_load = local(coupling_any, coupling, w_sem.at[1])
    top_load = local(top_any, top_c, w_sem.at[2])

    basis[...] = jnp.zeros_like(basis)
    for at, i in enumerate(IN_ORDER):
        for c in range(2):
            basis[pl.ds(at * 64 + c * 32, 32), pl.ds((i * 2 + c) * 256, 256)] = bt[...]
    paths = tree_paths(transfer)
    four = split(paths[3])
    merge_up = split(leaf_paths(paths[2], IN_ORDER, (0, 1)))
    rows = mask_rows(valid[...])
    for i in (0, 3, 1, 2):
        await_bytes(xs.at[i], x_sem.at[i])
        for c in range(2):
            col = column(rows[i : i + 1, c * 512 : c * 512 + 512]).astype(BF16)
            mcol[i, c] = col
            for lt in range(2):
                part = xs.at[i, c, lt].reshape(512, 128)[...]
                taps[i, c, 16:528, lt * 128 : lt * 128 + 128] = part * col
    pixels = jnp.concatenate([taps[i, c, 16:528] for i in range(4) for c in range(2)], 1)
    packed[...] = dot(pixels, basis[...], NT)
    top = climb(packed[...], v_ref, w_ref, merge_up, four)
    table[pl.ds(me, 1)] = jnp.concatenate([top[0:1], top[1:2], jnp.zeros((1, 64), F32)], 1).reshape(1, 1, 128)

    pl.semaphore_wait(barrier, 2 + 15 + groups - 1)
    mine = table.at[pl.ds(me, 1)]
    for peer in peers1:
        remote(mine, mine, g_s.at[0], g_r.at[0], peer)
    for k in range(2):
        row = packed[:, 128 + 64 * k : 192 + 64 * k]
        outer[k] = jnp.concatenate([row[0:256], row[256:512]], 1)
    inner_rows[...] = packed[:, 0:128]
    coef_copies = [
        remote(inner_rows, hc.at[0], cf_s.at[0], cf_r.at[0], right),
        remote(inner_rows, hc.at[1], cf_s.at[1], cf_r.at[1], left),
        remote(outer.at[1], ho.at[0], cf_s.at[2], cf_r.at[2], right),
        remote(outer.at[0], ho.at[1], cf_s.at[3], cf_r.at[3], left),
    ]
    inside = pl.ds(16, 512)
    to_right = remote_copy(taps.at[3, pl.ds(0, 2), inside], hx.at[0], px_s.at[0], px_r.at[0], right)
    to_left = remote_copy(taps.at[0, pl.ds(0, 2), inside], hx.at[1], px_s.at[1], px_r.at[1], left)

    @pl.when(core == 0)
    def _():
        to_right.start()

    @pl.when(core == 1)
    def _():
        to_left.start()

    weight[...] = jnp.zeros_like(weight)
    for i2 in range(2):
        for c in range(2):
            start = (1 - i2) * 64 + (1 - c) * 32
            weight[i2, c, pl.ds(start, 32)] = bt[...]
            weight[i2, c, pl.ds(128 + start, 32)] = bt[...]
    for r in range(4):
        shifted(taps, r)
    near_load.wait()
    near_out[...] = near[pl.ds(pl.multiple_of(1536 * core, 256), 768)]
    near_rows(taps, near, acc, 1, (0, 1, 2), False)
    near_rows(taps, near, acc, 2, (0, 1, 2), False)
    near_rows(taps, near, acc, 0, (1, 2), False)
    near_rows(taps, near, acc, 3, (0, 1), False)
    coupling_load.wait()
    far_weights(coupling, blocks, window, w_hi, w_lo)

    await_bytes(table.at[pl.ds(0, 15)], g_r.at[0])
    block = table.at[pl.ds(group * 16, 16)]
    for peer in peers2:
        remote(block, block, g_s.at[1], g_r.at[1], peer)

    @pl.when(core == 1)
    def _():
        to_right.start()

    @pl.when(core == 0)
    def _():
        to_left.start()

    coef[0:8] = jnp.zeros((8, 256), F32)
    coef[520:528] = jnp.zeros((8, 256), F32)
    coef[8:520] = packed[...]
    far_field(coef, 0, w_hi, w_lo, far)
    top_load.wait()
    slots = top_blocks(me, offset_t, top_c)
    pick = top_picks(me, partner_t, count)
    stacks = (None,) + tuple(split(path) for path in paths[:3])
    roots = split(root_paths(me, paths, path_ref))
    merge_down = split(leaf_paths(paths[2], (3, 2, 1, 0), (1, 0)))

    await_bytes(hx.at[0], px_r.at[edge])
    edge_taps[0, 0, inside] = hx[edge, 0]
    edge_taps[0, 1, inside] = hx[edge, 1]
    shifted(edge_taps, 0)
    for c in range(2):
        for m in range(512 // CHUNK):
            parts = [edge_taps[0, ORDER[c][b], pl.ds(16 + m * CHUNK, CHUNK)] for b in range(3)]
            rows = pl.ds(m * CHUNK, CHUNK)
            begin = pl.multiple_of(1536 * edge, 256)
            acc[3 * edge, c, rows] += dot(jnp.concatenate(parts, 1), near[pl.ds(begin, 768)])

    for copy in coef_copies:
        copy.wait()
    coef_halo[0:8] = jnp.zeros((8, 384), F32)
    coef_halo[520:528] = jnp.zeros((8, 384), F32)
    for k, inner in enumerate((jnp.where(me > 0, 1.0, 0.0), jnp.where(me < n - 1, 1.0, 0.0))):
        coef_halo[8:520, 128 * k : 128 * k + 128] = hc[k] * inner
        start = 256 + 64 * k
        row = ho[k] * inner
        coef_halo[8:264, start : start + 64] = row[:, 0:64]
        coef_halo[264:520, start : start + 64] = row[:, 64:128]
    far_field(coef_halo, 1024, w_hi, w_lo, far)

    await_bytes(table.at[pl.ds(0, n - 16)], g_r.at[1])
    local_exp = top_expand(table.reshape(n, 128)[...], pick, slots, stacks)
    leaf = descend(local_exp, v_ref, w_ref, roots, four, merge_down) + far[...]
    hi, lo = split(leaf)
    for half in range(2):
        exps[half, :, 0:128] = hi[:, half * 128 : half * 128 + 128]
        exps[half, :, 128:256] = lo[:, half * 128 : half * 128 + 128]
    await_bytes(hx.at[0], px_r.at[core])
    await_bytes(hx.at[0], px_s.at[0])
    await_bytes(hx.at[0], px_s.at[1])
    await_bytes(table.at[pl.ds(0, 15)], g_s.at[0])
    await_bytes(table.at[pl.ds(0, n - 16)], g_s.at[1])


def kernel_out(n, acc, exps, mcol, hx, weight, near, out, taps, os, out_sem):
    me = lax.axis_index("region")
    edge = lax.rem(me, 2)
    for at, (i, side) in enumerate(((1, 1), (2, 0), (3 - 3 * edge, 1 - edge), (3 * edge, edge))):
        half = 1 - side if at >= 2 else 1 - i // 2
        if at == 3:
            inner = jnp.where(edge == 0, me > 0, me < n - 1).astype(F32).astype(BF16)
            for c in range(2):
                taps[0, c, 16:528] = hx[edge, c] * inner
            shifted(taps, 0)
        for c in range(2):
            total = acc[i, c] + dot(exps[half], weight[side, c])
            if at == 3:
                parts = [taps[0, ORDER[c][b], 16:528] for b in range(3)]
                total = total + dot(jnp.concatenate(parts, 1), near[...])
            col = mcol[i, c].astype(F32)
            for lt in range(2):
                os.at[at, c, lt].reshape(512, 128)[...] = total[:, lt * 128 : lt * 128 + 128] * col
                local(os.at[at, c, lt], out.at[i, :, c, :, pl.ds(lt * 128, 128)], out_sem.at[0])
    await_bytes(os, out_sem.at[0])


def body(n, pixels, valid, basis, near, transfer, coupling, top_c, partner, offset, count):
    x = pixels.reshape(4, 256, 2, 2, 256)
    bt = basis.T
    near = near.reshape(2304, 256)
    vmem = pl.BlockSpec(memory_space=pltpu.VMEM)
    anywhere = pl.BlockSpec(memory_space=pl.ANY)
    sds = jax.ShapeDtypeStruct
    dma = pltpu.SemaphoreType.DMA
    passed = pl.pallas_call(
        functools.partial(kernel_main, n),
        out_shape=(
            pltpu.VMEM((4, 2, 512, 256), F32), pltpu.VMEM((2, 512, 256), BF16), pltpu.VMEM((4, 2, 512, 128), BF16),
            pltpu.VMEM((2, 2, 512, 256), BF16),
            pltpu.VMEM((2, 2, 256, 256), BF16),
            pltpu.VMEM((768, 256), BF16),
        ),
        in_specs=[anywhere] * 4 + [vmem] * 5 + [pl.BlockSpec(memory_space=pltpu.SMEM)],
        out_specs=(vmem,) * 6,
        scratch_shapes=[
            pltpu.VMEM((4, 2, 2, 256, 2, 128), BF16),
            pltpu.VMEM((2304, 256), BF16),
            pltpu.VMEM((32, 32, 40), F32),
            pltpu.VMEM((32, 32, 160), F32),
            pltpu.VMEM((4, 4, 544, 256), BF16),
            pltpu.VMEM((1, 4, 544, 256), BF16),
            pltpu.VMEM((256, 2048), BF16),
            pltpu.VMEM((512, 256), F32),
            pltpu.VMEM((512, 128), F32),
            pltpu.VMEM((2, 256, 128), F32),
            pltpu.VMEM((528, 256), F32),
            pltpu.VMEM((528, 384), F32),
            pltpu.VMEM((2, 512, 128), F32),
            pltpu.VMEM((2, 256, 128), F32),
            pltpu.VMEM((n, 1, 128), F32),
            pltpu.VMEM((1280, 128), F32),
            pltpu.VMEM((2, 8, 32, 1024), F32),
            pltpu.VMEM((2560, 256), BF16),
            pltpu.VMEM((2560, 256), BF16),
            pltpu.VMEM((512, 256), F32),
            pltpu.VMEM((512, 128), F32),
            pltpu.VMEM((32, 128), F32),
            pltpu.VMEM((448, 128), F32),
            dma((4,)),
            dma((3,)),
            dma((4,)),
            dma((4,)),
            dma((4,)),
            dma((4,)),
            dma((2,)),
            dma((2,)),
        ],
        compiler_params=pltpu.CompilerParams(collective_id=0, has_side_effects=True, vmem_limit_bytes=VMEM_LIMIT),
    )(
        x, near, jnp.transpose(coupling, (1, 2, 0)), jnp.transpose(top_c, (1, 2, 0)),
        valid, bt, transfer, partner.T, offset.T, count,
    )
    out = pl.pallas_call(
        functools.partial(kernel_out, n),
        out_shape=sds((4, 256, 2, 2, 256), F32),
        in_specs=[vmem] * 6,
        out_specs=anywhere,
        scratch_shapes=[
            pltpu.VMEM((1, 4, 544, 256), BF16),
            pltpu.VMEM((4, 2, 2, 256, 2, 128), F32),
            dma((1,)),
        ],
        compiler_params=pltpu.CompilerParams(vmem_limit_bytes=24 << 20),
    )(*(pltpu.with_memory_space_constraint(a, pltpu.VMEM) for a in passed))
    return out.reshape(4, 512, 2, 256)


def solution(mesh):
    n = mesh.shape["region"]
    in_specs = (P("region", None, None, None), P("region", None)) + (P(),) * 8
    out_specs = P("region", None, None, None)
    return jax.shard_map(functools.partial(body, n), mesh=mesh, in_specs=in_specs, out_specs=out_specs, check_vma=False)
```
